32 devices in a mesh: segment: 4 (over z), expert: 8 (over y, x, core).
Axes of the slice: x: 2, y: 2, z: 4, core: 2. Of those that a mesh axis runs over, the one named last changes fastest.
Arguments:
- section_output: bfloat16 [4, 512, 2048], P('segment', 'expert'), may hold values from -6 to 6
- section_gradient: bfloat16 [4, 512, 2048], P('segment', 'expert'), may hold values from -6 to 6
- forward_routes: int32 [4, 512, 8], P('segment', 'expert'), may hold values from 0 to 127, all different within a row; in each aligned block of 64 rows (0 to 63, 64 to 127, ..., all dimensions but the last counted through in order) at most 5 rows name the same one
- forward_logits: float32 [4, 512, 8], P('segment', 'expert'), may hold values from -1.2 to 1.2
- backward_routes: int32 [4, 512, 8], P('segment', 'expert'), may hold values from 0 to 127, all different within a row; in each aligned block of 64 rows (0 to 63, 64 to 127, ..., all dimensions but the last counted through in order) at most 5 rows name the same one
- backward_logits: float32 [4, 512, 8], P('segment', 'expert'), may hold values from -1.2 to 1.2
- entry_weights: bfloat16 [4, 8, 2048, 384], P('segment', 'expert'), may hold values from -0.25 to 0.25
- down_weights: bfloat16 [4, 8, 192, 2048], P('segment', 'expert'), may hold values from -0.3125 to 0.3125
- saved_projections: bfloat16 [4, 8, 40, 384], P('segment', 'expert'), may hold values from -8 to 8
Outputs:
- forward_output: bfloat16 [4, 512, 2048], P('segment', 'expert')
- input_gradient: bfloat16 [4, 512, 2048], P('segment', 'expert')
The draws below stay inside these ranges and needn't reach their ends.
Inputs may be any that keep to these rules, and one draw needn't show every extreme that they name: `forward_routes`: each token's 8 ids differ. Within one device's 64 tokens of a section (aligned blocks) no expert is named by more than 5 routes, and some block has an expert named by exactly 5. `backward_routes`: each token's 8 ids differ. Within one device's 64 tokens of a section (aligned blocks) no expert is named by more than 5 routes, and some block has an expert named by exactly 5.
All inputs are finite; a program needn't handle non-finite values.
Results may differ from the reference program's by a relative error of at most 0.0038.
Values may be sent and summed in bfloat16 or wider, within the bound.
No kernel may reach another device: no remote copies, remote signals or barrier semaphores. Data moves between devices by JAX's collectives and lax.ppermute only.
A program may use at most 64 MiB of HBM per device.

```python
import math
import jax
import jax.numpy as jnp
import numpy as np
from jax import lax

D = 2048
FF = 1536
EXPERTS = 128
TOP = 8
FSPLIT = 8
TOK_DEV = 64
HID = 192
EXP_WIN = 1
CAP = 5
SEGMENTS = 4
TOKENS = 512
N_EXPERT = 8


def block_scale(rng, extent, split, low, largest):
    def one(axis_at, parts):
        heights = jax.random.uniform(jax.random.fold_in(jax.random.fold_in(rng, 6), axis_at), (parts,), jnp.float32, low / len(split), largest / len(split))
        return jnp.repeat(jnp.exp(heights), extent[axis_at] // parts).reshape((-1,) + (1,) * (len(extent) - axis_at - 1))

    factor_of = one(*split[0])
    for cut in split[1:]:
        factor_of = factor_of * one(*cut)
    return factor_of


def shared_out(rng, own, number, rows, amount, top, most, slope):
    ranking = jax.random.permutation(rng, amount)
    crowded, common = portions_of(amount, rows * top, most, slope, True), portions_of(amount, rows * top, most, slope, False)
    places = jnp.arange(amount)

    def named(tallies, offset_by):
        used = int((tallies > 0).sum())
        fixed = max(1, used // 4)
        passed = fixed + (places - fixed + offset_by * (used - fixed)) % max(1, amount - fixed)
        return jnp.zeros((amount,), jnp.int32).at[ranking[jnp.where(places < fixed, places, passed)]].set(jnp.asarray(tallies, jnp.int32))

    tallies = jnp.where(number % 4 == 0, named(crowded, number // 4), named(common, number - number // 4 - 1))
    mixed = jax.random.permutation(jax.random.fold_in(own, 3), amount)
    giver, receiver = mixed[0:amount // 2 * 2:2], mixed[1:amount // 2 * 2:2]
    room = jnp.minimum(tallies[giver] - 1, most - tallies[receiver]) // 2
    room = jnp.where((giver == ranking[0]) | (receiver == ranking[0]) | (tallies[receiver] == 0), 0, jnp.maximum(room, 0))
    passed = jax.random.randint(jax.random.fold_in(own, 4), (amount // 2,), 0, 1 << 20) % (room + 1)
    tallies = tallies.at[giver].add(-passed).at[receiver].add(passed)
    items = jnp.searchsorted(jnp.cumsum(tallies), jnp.arange(rows * top), side="right").astype(jnp.int32)
    listing = items.reshape(top, rows).T
    listing = listing[jax.random.permutation(jax.random.fold_in(own, 1), rows)]
    offset_by = jax.random.randint(jax.random.fold_in(own, 2), (rows, 1), 0, top)
    return jnp.take_along_axis(listing, (jnp.arange(top)[None, :] + offset_by) % top, axis=1)


def portions_of(number_of, total, reach, lean, full):
    loads = [(1 << 20) // math.isqrt(grade ** lean) + 1 for grade in range(1, number_of + 1)]
    largest = reach if full else min(reach, max(-(-total // number_of), total * loads[0] // sum(loads)))
    least = 1 if total - largest >= number_of - 1 else 0
    counts, spare = [largest] + [least] * (number_of - 1), total - largest - least * (number_of - 1)
    while spare > 0:
        free = [i for i in range(1, number_of) if counts[i] < largest] or [i for i in range(1, number_of) if counts[i] < reach]
        mass, budget = sum([loads[i] for i in free]), spare
        for i in free:
            addition = min(reach - counts[i], max(1, budget * loads[i] // mass), spare)
            counts[i] = counts[i] + addition
            spare = spare - addition
    return np.array(counts)


def gaussian(key, dims, spread, limit, shards=(), kind=jnp.bfloat16):
    drawn = spread * jax.random.normal(key, dims, jnp.float32)
    if shards:
        drawn = drawn * block_scale(key, dims, shards, -0.22, 0.18)
    return jnp.clip(drawn, -limit, limit).astype(kind)


def setup_inputs(seed: int = 0) -> dict:
    arg_keys = jax.random.split(jax.random.key(seed), 10)
    section_output = gaussian(arg_keys[0], (SEGMENTS, TOKENS, D), 1.0, 6.0, ((0, 4), (1, 8)))
    section_gradient = gaussian(arg_keys[1], (SEGMENTS, TOKENS, D), 1.0, 6.0, ((0, 4), (1, 8)))
    forward_routes_keys = jax.random.split(jax.random.fold_in(arg_keys[2], 1), SEGMENTS * TOKENS // TOK_DEV)
    forward_routes_turns = jax.random.permutation(jax.random.fold_in(arg_keys[2], 3), SEGMENTS * TOKENS // TOK_DEV)
    forward_routes = jax.vmap(lambda own, number: shared_out(jax.random.fold_in(arg_keys[2], 2), own, number, TOK_DEV, EXPERTS, TOP, CAP, 2))(forward_routes_keys, forward_routes_turns).reshape((SEGMENTS, TOKENS, TOP))
    forward_logits = jnp.clip(jax.random.uniform(arg_keys[3], (SEGMENTS, TOKENS, TOP), jnp.float32, -1.2, 1.2) * block_scale(arg_keys[3], (SEGMENTS, TOKENS, TOP), ((0, 4), (1, 8)), -0.4, 0.0), -1.2, 1.2)
    backward_routes_keys = jax.random.split(jax.random.fold_in(arg_keys[4], 1), SEGMENTS * TOKENS // TOK_DEV)
    backward_routes_turns = jax.random.permutation(jax.random.fold_in(arg_keys[4], 3), SEGMENTS * TOKENS // TOK_DEV)
    backward_routes = jax.vmap(lambda own, number: shared_out(jax.random.fold_in(arg_keys[4], 2), own, number, TOK_DEV, EXPERTS, TOP, CAP, 2))(backward_routes_keys, backward_routes_turns).reshape((SEGMENTS, TOKENS, TOP))
    backward_logits = jnp.clip(jax.random.uniform(arg_keys[5], (SEGMENTS, TOKENS, TOP), jnp.float32, -1.2, 1.2) * block_scale(arg_keys[5], (SEGMENTS, TOKENS, TOP), ((0, 4), (1, 8)), -0.4, 0.0), -1.2, 1.2)
    entry_weights = gaussian(arg_keys[6], (SEGMENTS, N_EXPERT, D, 2 * HID), (D // 4) ** -0.5, 0.25, ((0, 4), (1, 8)))
    down_weights = gaussian(arg_keys[7], (SEGMENTS, N_EXPERT, HID, D), (FF // 4) ** -0.5, 0.3125, ((0, 4), (1, 8)))
    saved_projections = gaussian(arg_keys[8], (SEGMENTS, N_EXPERT, N_EXPERT * CAP, 2 * HID), 1.5, 8.0, ((0, 4), (1, 8)))
    return dict(section_output=section_output, section_gradient=section_gradient, forward_routes=forward_routes, forward_logits=forward_logits, backward_routes=backward_routes, backward_logits=backward_logits, entry_weights=entry_weights, down_weights=down_weights, saved_projections=saved_projections)


def rounded(values):
    return lax.optimization_barrier(values.astype(jnp.bfloat16)).astype(jnp.float32)


def slot_table(block_routes):
    flat_routes = block_routes.reshape(-1)
    expert_hit = (flat_routes[:, None] == jnp.arange(EXP_WIN, dtype=jnp.int32)[None, :]).astype(jnp.int32)
    earlier = jnp.cumsum(expert_hit, axis=0) - expert_hit
    picked = expert_hit[:, :, None] * (earlier[:, :, None] == jnp.arange(CAP, dtype=jnp.int32)[None, None, :]).astype(jnp.int32)
    return picked.reshape(flat_routes.shape[0], EXP_WIN * CAP).astype(jnp.float32)


def route_probs(logits):
    scores = jnp.exp(logits)
    return scores / jnp.sum(scores, axis=-1, keepdims=True)


def owner_rows(tables, route_rows):
    slots = jnp.einsum("prs,prd->psd", tables, route_rows, precision=lax.Precision.HIGHEST)
    slots = slots.reshape(N_EXPERT, EXP_WIN, CAP, D)
    return jnp.repeat(slots, FSPLIT, axis=1)


def returned_rows(tables, partials):
    summed = jnp.sum(partials.reshape(N_EXPERT, EXP_WIN, FSPLIT, CAP, D), axis=2)
    summed = summed.reshape(N_EXPERT, EXP_WIN * CAP, D)
    return jnp.einsum("prs,psd->prd", tables, summed, precision=lax.Precision.HIGHEST)


def forward_section(layer_input, routes, logits, entry, down):
    tables = jax.vmap(slot_table)(routes.reshape(N_EXPERT, TOK_DEV, TOP))
    repeated = jnp.repeat(layer_input.astype(jnp.float32).reshape(N_EXPERT, TOK_DEV, D), TOP, axis=1)
    arrived = owner_rows(tables, repeated)
    preacts = jnp.einsum("pocd,odk->pock", arrived, entry.astype(jnp.float32), precision=lax.Precision.HIGHEST)
    gate = preacts[..., :HID]
    upper = preacts[..., HID:]
    hidden = rounded(gate * jax.nn.sigmoid(gate) * upper)
    partials = rounded(jnp.einsum("pock,okd->pocd", hidden, down.astype(jnp.float32), precision=lax.Precision.HIGHEST))
    route_out = returned_rows(tables, partials).reshape(N_EXPERT, TOK_DEV, TOP, D)
    probs = route_probs(logits).reshape(N_EXPERT, TOK_DEV, TOP)
    branch = jnp.sum(route_out * probs[..., None], axis=2).reshape(TOKENS, D)
    return (layer_input.astype(jnp.float32) + branch).astype(jnp.bfloat16)


def backward_section(upstream, routes, logits, entry, down, saved):
    tables = jax.vmap(slot_table)(routes.reshape(N_EXPERT, TOK_DEV, TOP))
    probs = route_probs(logits).reshape(N_EXPERT, TOK_DEV * TOP)
    repeated = jnp.repeat(upstream.astype(jnp.float32).reshape(N_EXPERT, TOK_DEV, D), TOP, axis=1)
    scaled = rounded(repeated * probs[..., None])
    arrived = owner_rows(tables, scaled)
    stored = saved.astype(jnp.float32).reshape(N_EXPERT, N_EXPERT, CAP, 2 * HID).transpose(1, 0, 2, 3)
    gate = stored[..., :HID]
    upper = stored[..., HID:]
    grad_hidden = jnp.einsum("pocd,ohd->poch", arrived, down.astype(jnp.float32), precision=lax.Precision.HIGHEST)
    logistic = jax.nn.sigmoid(gate)
    grad_gate = grad_hidden * upper * logistic * (1.0 + gate * (1.0 - logistic))
    grad_upper = grad_hidden * gate * logistic
    grad_pre = rounded(jnp.concatenate([grad_gate, grad_upper], axis=-1))
    partials = rounded(jnp.einsum("pock,odk->pocd", grad_pre, entry.astype(jnp.float32), precision=lax.Precision.HIGHEST))
    route_back = returned_rows(tables, partials).reshape(N_EXPERT, TOK_DEV, TOP, D)
    total = jnp.sum(route_back, axis=2).reshape(TOKENS, D)
    return (upstream.astype(jnp.float32) + total).astype(jnp.bfloat16)


def forward_packed(packed):
    return forward_section(*packed)


def backward_packed(packed):
    return backward_section(*packed)


def reference(section_output, section_gradient, forward_routes, forward_logits, backward_routes, backward_logits, entry_weights, down_weights, saved_projections):
    inputs = jnp.roll(section_output, 1, axis=0)
    upstreams = jnp.roll(section_gradient, -1, axis=0)
    forward_output = lax.map(forward_packed, (inputs, forward_routes, forward_logits, entry_weights, down_weights))
    input_gradient = lax.map(backward_packed, (upstreams, backward_routes, backward_logits, entry_weights, down_weights, saved_projections))
    return forward_output, input_gradient
```

```python
import functools

import jax
import jax.numpy as jnp
from jax import lax
from jax.experimental import pallas as pl
from jax.experimental.pallas import tpu as pltpu
from jax.sharding import PartitionSpec as P

FSPLIT = 8
CAP = 5
CORES = 2
SLOTS = 8
PAIR = 2 * SLOTS
MIB = 1 << 20


def along_sections(value, steps):
    count = lax.axis_size("segment")
    pairs = [(source, (source + steps) % count) for source in range(count)]
    return lax.ppermute(value, "segment", pairs)


def across_owners(value, flip):
    count = lax.axis_size("expert")
    return lax.ppermute(value, "expert", [(source, source ^ flip) for source in range(count)])


def in_vmem(count):
    return [pl.BlockSpec(memory_space=pltpu.VMEM)] * count


def call(kernel, outs, args, limit, flops, moved):
    return pl.pallas_call(
        kernel,
        out_shape=outs,
        in_specs=in_vmem(len(args)),
        out_specs=jax.tree.map(lambda _: pl.BlockSpec(memory_space=pltpu.VMEM), outs),
        compiler_params=pltpu.CompilerParams(vmem_limit_bytes=limit),
        cost_estimate=pl.CostEstimate(flops=flops, bytes_accessed=moved, transcendentals=0),
    )(*args)


def dot(left, right):
    return jnp.dot(left, right, preferred_element_type=jnp.float32)


def dot_rows(left, right):
    return lax.dot_general(left, right, (((1,), (1,)), ((), ())), preferred_element_type=jnp.float32)


def prepare_kernel(
    groups,
    chips,
    mixed,
    routes_a,
    logits_a,
    routes_b,
    logits_b,
    saved_own,
    saved_pair,
    pick_x,
    pick_u,
    place_x,
    place_u,
    send_scale,
    sum_scale,
    *factors,
):
    toks = routes_a.shape[1]
    top = routes_a.shape[2]
    before = lax.broadcasted_iota(jnp.int32, (toks, toks), 0) < lax.broadcasted_iota(
        jnp.int32, (toks, toks), 1
    )
    before = before.astype(jnp.float32).astype(jnp.bfloat16)
    after = lax.broadcasted_iota(jnp.int32, (toks, toks), 0) > lax.broadcasted_iota(
        jnp.int32, (toks, toks), 1
    )
    after = after.astype(jnp.float32).astype(jnp.bfloat16)
    row = lax.broadcasted_iota(jnp.int32, (PAIR, toks), 0)
    lane = lax.broadcasted_iota(jnp.int32, (toks, place_x.shape[1]), 1)
    half_row = lax.broadcasted_iota(jnp.int32, (PAIR, 128), 0)
    ones = jnp.ones((PAIR, top), jnp.bfloat16)

    def micro(routes, logits, offset):
        scores = jnp.exp(logits[0])
        probs = scores / jnp.sum(scores, axis=1, keepdims=True)
        picks, scales = [], []
        place = jnp.zeros((toks, place_x.shape[1]), jnp.float32)
        for group in range(groups):
            hit = (routes[0] == group).astype(jnp.float32)
            along = dot_rows(ones, hit.astype(jnp.bfloat16))
            rank = dot(along.astype(jnp.bfloat16), before)
            pick = jnp.where(rank == (row - offset).astype(jnp.float32), along, 0.0)
            prob = jnp.sum(hit * probs, axis=1, keepdims=True)
            scales.append(
                jnp.dot(
                    pick,
                    jnp.broadcast_to(prob, (toks, 128)),
                    preferred_element_type=jnp.float32,
                    precision=lax.Precision.HIGHEST,
                )
            )
            picks.append(pick)
            down = jnp.broadcast_to(jnp.sum(hit, axis=1, keepdims=True), place.shape)
            down_rank = dot(after, down.astype(jnp.bfloat16))
            spot = lane % (groups * PAIR) - group * PAIR - offset
            place = place + jnp.where(down_rank == spot.astype(jnp.float32), down, 0.0)
        return picks, scales, place

    picks_a, scales_a, place_a = micro(routes_a, logits_a, 0)
    picks_b, scales_b, place_b = micro(routes_b, logits_b, SLOTS)
    for group in range(groups):
        rows = pl.ds(group * PAIR, PAIR)
        pick_x[rows, :] = picks_a[group].astype(jnp.bfloat16)
        pick_u[rows, :] = picks_b[group].astype(jnp.bfloat16)
        send_scale[rows, :] = jnp.where(half_row < SLOTS, 1.0, scales_b[group])
        sum_scale[rows, :] = jnp.where(half_row < SLOTS, scales_a[group], 1.0)
    place_x[...] = place_a.astype(jnp.bfloat16)
    place_u[...] = place_b.astype(jnp.bfloat16)

    me = lax.axis_index("expert")
    held = saved_own.shape[2]
    line = lax.broadcasted_iota(jnp.int32, (chips * PAIR, held), 0)
    origin = line // PAIR
    if mixed:
        origin = origin ^ (me // CORES)
    slot = line % PAIR - SLOTS
    wanted = (CORES * origin + me % CORES) * CAP + slot
    wanted = jnp.where((slot >= 0) & (slot < CAP), wanted, -1)
    chosen = (wanted == lax.broadcasted_iota(jnp.int32, (chips * PAIR, held), 1)).astype(jnp.float32)
    chosen = chosen.astype(jnp.bfloat16)
    for owner, saved in enumerate((saved_own, saved_pair)):
        stored = dot(chosen, saved[0, 0])
        half = stored.shape[1] // 2
        gate = stored[:, :half]
        upper = stored[:, half:]
        logistic = jax.nn.sigmoid(gate)
        factors[owner][:, :half] = upper * logistic * (1.0 + gate * (1.0 - logistic))
        factors[owner][:, half:] = gate * logistic


def select_kernel(groups, x, u, pick_x, pick_u, send_scale, message):
    for group in range(groups):
        rows = pl.ds(group * PAIR, PAIR)
        chosen = dot(pick_x[rows, :], x[0]) + dot(pick_u[rows, :], u[0])
        message[group] = (chosen * send_scale[rows, :1]).astype(jnp.bfloat16)


def expert_kernel(chips, *refs):
    arrived = refs[:chips]
    entries = refs[chips : chips + 2]
    downs = refs[chips + 2 : chips + 4]
    factors = refs[chips + 4 : chips + 6]
    results = refs[chips + 6 :]
    rows = jnp.concatenate([ref[...] for ref in arrived], axis=0)
    total = None
    for entry, down, factor in zip(entries, downs, factors):
        half = down.shape[2]
        preacts = dot(rows, entry[0, 0])
        back = dot_rows(rows, down[0, 0])
        half = back.shape[1]
        line = lax.broadcasted_iota(jnp.int32, back.shape, 0) % PAIR
        gate = preacts[:, :half]
        hidden = gate * jax.nn.sigmoid(gate) * preacts[:, half:]
        hidden = jnp.where(line < SLOTS, hidden, 0.0).astype(jnp.bfloat16)
        grads = (jnp.concatenate([back, back], axis=1) * factor[...]).astype(jnp.bfloat16)
        part = dot(hidden, down[0, 0]) + dot_rows(grads, entry[0, 0])
        total = part if total is None else total + part
    total = total.astype(jnp.bfloat16)
    for index, ref in enumerate(results):
        ref[...] = total[index * PAIR : (index + 1) * PAIR]


def finish_kernel(groups, chips, *refs):
    x, u, place_x, place_u, sum_scale = refs[:5]
    returned = refs[5 : 5 + chips]
    out_x, out_u = refs[5 + chips :]
    share = chips // groups
    sums = []
    for group in range(groups):
        total = returned[group * share][...].astype(jnp.float32)
        for ref in returned[group * share + 1 : (group + 1) * share]:
            total = total + ref[...].astype(jnp.float32)
        sums.append(total * sum_scale[pl.ds(group * PAIR, PAIR), :1])
    rest = sums[0] if groups == 1 else jnp.concatenate(sums, axis=0)
    pieces = []
    for _ in range(3):
        piece = rest.astype(jnp.bfloat16)
        pieces.append(piece)
        rest = rest - piece.astype(jnp.float32)
    pieces = jnp.concatenate(pieces, axis=0)
    out_x[0] = (x[0].astype(jnp.float32) + dot(place_x[...], pieces)).astype(jnp.bfloat16)
    out_u[0] = (u[0].astype(jnp.float32) + dot(place_u[...], pieces)).astype(jnp.bfloat16)


def shards(
    section_output,
    section_gradient,
    forward_routes,
    forward_logits,
    backward_routes,
    backward_logits,
    entry_weights,
    down_weights,
    saved_projections,
):
    owners = lax.axis_size("expert")
    groups = owners // FSPLIT
    chips = owners // CORES
    direct = chips == 4
    toks, width = section_output.shape[1:]
    half = down_weights.shape[2]
    shape = jax.ShapeDtypeStruct
    bf16, f32 = jnp.bfloat16, jnp.float32

    layer_input = along_sections(section_output, 1)
    upstream = along_sections(section_gradient, -1)
    saved_pair = across_owners(saved_projections, 1)
    entry_pair = across_owners(entry_weights, 1)
    down_pair = across_owners(down_weights, 1)

    prepared = call(
        functools.partial(prepare_kernel, groups, chips, direct),
        (
            shape((groups * PAIR, toks), bf16),
            shape((groups * PAIR, toks), bf16),
            shape((toks, 3 * groups * PAIR), bf16),
            shape((toks, 3 * groups * PAIR), bf16),
            shape((groups * PAIR, 128), f32),
            shape((groups * PAIR, 128), f32),
            shape((chips * PAIR, 2 * half), f32),
            shape((chips * PAIR, 2 * half), f32),
        ),
        (
            forward_routes,
            forward_logits,
            backward_routes,
            backward_logits,
            saved_projections,
            saved_pair,
        ),
        8 * MIB,
        10_000_000,
        1_000_000,
    )
    pick_x, pick_u, place_x, place_u, send_scale, sum_scale, factor_own, factor_pair = prepared

    message = call(
        functools.partial(select_kernel, groups),
        shape((groups, PAIR, width), bf16),
        (layer_input, upstream, pick_x, pick_u, send_scale),
        8 * MIB,
        10_000_000,
        1_000_000,
    )
    if direct:
        arrived = [message[0]] + [across_owners(message[0], CORES * flip) for flip in range(1, chips)]
    else:
        same_core = [list(range(core, owners, CORES)) for core in range(CORES)]
        spread = jnp.repeat(message, chips // groups, axis=0)
        gathered = lax.all_to_all(
            spread, "expert", 0, 0, axis_index_groups=same_core, tiled=True
        )
        arrived = [gathered[index] for index in range(chips)]
    results = call(
        functools.partial(expert_kernel, chips),
        (shape((PAIR, width), bf16),) * chips,
        (
            *arrived,
            entry_weights,
            entry_pair,
            down_weights,
            down_pair,
            factor_own,
            factor_pair,
        ),
        24 * MIB,
        800_000_000,
        5_000_000,
    )
    if direct:
        returned = [results[0]] + [
            across_owners(results[flip], CORES * flip) for flip in range(1, chips)
        ]
    else:
        gathered = lax.all_to_all(
            jnp.stack(results), "expert", 0, 0, axis_index_groups=same_core, tiled=True
        )
        returned = [gathered[index] for index in range(chips)]
    return call(
        functools.partial(finish_kernel, groups, chips),
        (shape((1, toks, width), bf16), shape((1, toks, width), bf16)),
        (layer_input, upstream, place_x, place_u, sum_scale, *returned),
        16 * MIB,
        10_000_000,
        1_000_000,
    )


def solution(mesh):
    rows = P("segment", "expert", None)
    blocks = P("segment", "expert", None, None)
    return jax.shard_map(
        shards,
        mesh=mesh,
        in_specs=(rows,) * 6 + (blocks,) * 3,
        out_specs=(rows, rows),
        check_vma=False,
    )
```

```python
import functools

import jax
import jax.numpy as jnp
from jax import lax
from jax.experimental import pallas as pl
from jax.experimental.pallas import tpu as pltpu
from jax.sharding import PartitionSpec as P

FSPLIT = 8
CAP = 5
CORES = 2
SLOTS = 8
PAIR = 2 * SLOTS
MIB = 1 << 20


def along_sections(value, steps):
    count = lax.axis_size("segment")
    pairs = [(source, (source + steps) % count) for source in range(count)]
    return lax.ppermute(value, "segment", pairs)


def across_owners(value, flip):
    count = lax.axis_size("expert")
    return lax.ppermute(value, "expert", [(source, source ^ flip) for source in range(count)])


def call(kernel, outs, args, limit, flops, moved, after=(), aliases=None, far=(), scratch=()):
    whole = pl.BlockSpec(memory_space=pltpu.VMEM)
    anywhere = pl.BlockSpec(memory_space=pl.ANY)
    distant = pl.BlockSpec(memory_space=pltpu.HBM)
    waits = len(after)

    def body(*refs):
        kernel(*refs[waits:])

    return pl.pallas_call(
        body,
        out_shape=outs,
        in_specs=[anywhere] * waits + [distant] * len(far) + [whole] * len(args),
        out_specs=jax.tree.map(lambda _: whole, outs),
        scratch_shapes=scratch,
        input_output_aliases={
            waits + len(far) + key: value for key, value in (aliases or {}).items()
        },
        compiler_params=pltpu.CompilerParams(vmem_limit_bytes=limit),
        cost_estimate=pl.CostEstimate(flops=flops, bytes_accessed=moved, transcendentals=0),
    )(*after, *[pltpu.with_memory_space_constraint(value, pltpu.HBM) for value in far], *args)


def dot(left, right):
    return jnp.dot(left, right, preferred_element_type=jnp.float32)


def hits(routes, group):
    return jnp.where(routes == group, 1.0, 0.0)


def slot_picks(routes, group, rows, offset):
    toks = routes.shape[1]
    shape = (toks, toks)
    before = lax.broadcasted_iota(jnp.int32, shape, 0) < lax.broadcasted_iota(jnp.int32, shape, 1)
    before = jnp.where(before, 1.0, 0.0).astype(jnp.bfloat16)
    along = jnp.sum(hits(routes, group), axis=0, keepdims=True)
    along = jnp.broadcast_to(along, (rows, toks))
    rank = dot(along.astype(jnp.bfloat16), before)
    slot = lax.broadcasted_iota(jnp.int32, (rows, toks), 0) - offset
    return jnp.where(rank == slot.astype(jnp.float32), along, 0.0)


def fetch(sources, targets, semaphores):
    copies = [
        pltpu.make_async_copy(source, target, semaphores.at[index])
        for index, (source, target) in enumerate(zip(sources, targets))
    ]
    for copy in copies:
        copy.start()
    for copy in copies:
        copy.wait()


def pick_kernel(groups, routes, staged, rows):
    picks = [slot_picks(routes[0], group, SLOTS, 0) for group in range(groups)]
    picks = picks[0] if groups == 1 else jnp.concatenate(picks, axis=0)
    rows[...] = dot(picks.astype(jnp.bfloat16), staged[0]).astype(jnp.bfloat16)


def merge_kernel(groups, x, pick_x, rows_b, send_scale, staged, message, whole):
    whole[...] = staged[...]
    all_a = dot(pick_x[...], x[0])
    all_b = rows_b[...].astype(jnp.float32)
    for group in range(groups):
        one = slice(group * SLOTS, (group + 1) * SLOTS)
        scaled = all_b[one] * send_scale[pl.ds(group * SLOTS, SLOTS), :1]
        both = [all_a[group * PAIR : group * PAIR + SLOTS], scaled]
        message[group] = jnp.concatenate(both, axis=0).astype(jnp.bfloat16)


def prepare_kernel(groups, *refs):
    far, refs = refs[:5], refs[5:]
    staged, pick_x, place_x, place_u, send_scale, sum_scale = refs[:6]
    near, semaphores, stage_semaphore = refs[6:10], refs[10], refs[11]
    stage = pltpu.make_async_copy(far[4], staged, stage_semaphore.at[0])
    stage.start()
    fetch(far[:4], near, semaphores)
    routes_a, logits_a, routes_b, logits_b = near

    def micro(routes, logits, offset):
        scores = jnp.exp(logits[0])
        probs = scores / jnp.sum(scores, axis=0, keepdims=True)
        picks, scales = [], []
        for group in range(groups):
            pick = slot_picks(routes[0], group, PAIR, offset)
            prob = jnp.sum(hits(routes[0], group) * probs, axis=0, keepdims=True)
            scales.append(jnp.sum(pick * prob, axis=1, keepdims=True))
            picks.append(pick)
        return picks, scales

    picks_a, scales_a = micro(routes_a, logits_a, 0)
    picks_b, scales_b = micro(routes_b, logits_b, SLOTS)
    place_x[...] = jnp.concatenate(picks_a * 3, axis=0).T.astype(jnp.bfloat16)
    place_u[...] = jnp.concatenate(picks_b * 3, axis=0).T.astype(jnp.bfloat16)
    half_row = lax.broadcasted_iota(jnp.int32, (PAIR, 128), 0)
    for group in range(groups):
        rows = pl.ds(group * PAIR, PAIR)
        pick_x[rows, :] = picks_a[group].astype(jnp.bfloat16)
        send_scale[pl.ds(group * SLOTS, SLOTS), :] = jnp.broadcast_to(
            scales_b[group][SLOTS:], (SLOTS, 128)
        )
        sum_scale[rows, :] = jnp.where(half_row < SLOTS, scales_a[group], 1.0)
    stage.wait()


def pack(index, chips, mixed, entry, down, saved, first, second, factors):
    half = down.shape[2]
    gate = slice(index * half, (index + 1) * half)
    upper = slice((2 + index) * half, (3 + index) * half)
    lower = slice((4 + index) * half, (5 + index) * half)
    first[:, gate] = entry[0, 0, :, :half]
    first[:, upper] = entry[0, 0, :, half:]
    first[:, lower] = down[0, 0].T
    second[gate, :] = entry[0, 0, :, :half].T
    second[upper, :] = entry[0, 0, :, half:].T
    second[lower, :] = down[0, 0]

    me = lax.axis_index("expert")
    held = saved.shape[2]
    shape = (chips * PAIR, held)
    line = lax.broadcasted_iota(jnp.int32, shape, 0)
    origin = line // PAIR
    if mixed:
        origin = origin ^ (me // CORES)
    slot = line % PAIR - SLOTS
    wanted = (CORES * origin + me % CORES) * CAP + slot
    wanted = jnp.where((slot >= 0) & (slot < CAP), wanted, -1)
    chosen = jnp.where(wanted == lax.broadcasted_iota(jnp.int32, shape, 1), 1.0, 0.0)
    stored = dot(chosen.astype(jnp.bfloat16), saved[0, 0])
    gates = stored[:, :half]
    uppers = stored[:, half:]
    logistic = jax.nn.sigmoid(gates)
    factors[:, gate] = uppers * logistic * (1.0 + gates * (1.0 - logistic))
    factors[:, upper] = gates * logistic


def pack_own_kernel(chips, mixed, *refs):
    far, packs, near, semaphores = refs[:3], refs[3:6], refs[6:9], refs[9]
    fetch(far, near, semaphores)
    pack(0, chips, mixed, *near, *packs)


def pack_pair_kernel(chips, mixed, *refs):
    pack(1, chips, mixed, *refs[:3], *refs[6:])


def expert_kernel(chips, *refs):
    arrived = refs[:chips]
    first, second, factors = refs[chips : chips + 3]
    results = refs[chips + 3 :]
    rows = jnp.concatenate([ref[...] for ref in arrived], axis=0)
    made = dot(rows, first[...])
    both = made.shape[1] // 3
    gate = made[:, :both]
    upper = made[:, both : 2 * both]
    back = made[:, 2 * both :]
    line = lax.broadcasted_iota(jnp.int32, back.shape, 0) % PAIR
    hidden = jnp.where(line < SLOTS, gate * jax.nn.sigmoid(gate) * upper, 0.0)
    grads = jnp.concatenate([back, back], axis=1) * factors[...]
    inner = jnp.concatenate([grads.astype(jnp.bfloat16), hidden.astype(jnp.bfloat16)], axis=1)
    total = dot(inner, second[...]).astype(jnp.bfloat16)
    for index, ref in enumerate(results):
        ref[...] = total[index * PAIR : (index + 1) * PAIR]


def finish_kernel(groups, chips, *refs):
    x, u, place_x, place_u, sum_scale = refs[:5]
    returned = refs[5 : 5 + chips]
    out_x, out_u = refs[5 + chips :]
    share = chips // groups
    sums = []
    for group in range(groups):
        total = returned[group * share][...].astype(jnp.float32)
        for ref in returned[group * share + 1 : (group + 1) * share]:
            total = total + ref[...].astype(jnp.float32)
        sums.append(total * sum_scale[pl.ds(group * PAIR, PAIR), :1])
    rest = sums[0] if groups == 1 else jnp.concatenate(sums, axis=0)
    pieces = []
    for _ in range(3):
        piece = rest.astype(jnp.bfloat16)
        pieces.append(piece)
        rest = rest - piece.astype(jnp.float32)
    pieces = jnp.concatenate(pieces, axis=0)
    out_x[0] = (x[0].astype(jnp.float32) + dot(place_x[...], pieces)).astype(jnp.bfloat16)
    out_u[0] = (u[0].astype(jnp.float32) + dot(place_u[...], pieces)).astype(jnp.bfloat16)


def shards(
    section_output,
    section_gradient,
    forward_routes,
    forward_logits,
    backward_routes,
    backward_logits,
    entry_weights,
    down_weights,
    saved_projections,
):
    owners = lax.axis_size("expert")
    groups = owners // FSPLIT
    chips = owners // CORES
    direct = chips == 4
    toks, width = section_output.shape[1:]
    half = down_weights.shape[2]
    shape = jax.ShapeDtypeStruct
    bf16, f32 = jnp.bfloat16, jnp.float32
    routes_a, logits_a, routes_b, logits_b = [
        jnp.swapaxes(value, 1, 2)
        for value in (forward_routes, forward_logits, backward_routes, backward_logits)
    ]

    block = shape((1, toks, width), bf16)
    asked = along_sections(routes_b, 1)
    layer_input = along_sections(section_output, 1)
    own_values = (routes_a, logits_a, routes_b, logits_b)
    staged, pick_x, place_x, place_u, send_scale, sum_scale = call(
        functools.partial(prepare_kernel, groups),
        (
            block,
            shape((groups * PAIR, toks), bf16),
            shape((toks, 3 * groups * PAIR), bf16),
            shape((toks, 3 * groups * PAIR), bf16),
            shape((groups * SLOTS, 128), f32),
            shape((groups * PAIR, 128), f32),
        ),
        (),
        8 * MIB,
        10_000_000,
        1_000_000,
        far=(*own_values, section_gradient),
        scratch=[
            *[pltpu.VMEM(value.shape, value.dtype) for value in own_values],
            pltpu.SemaphoreType.DMA((len(own_values),)),
            pltpu.SemaphoreType.DMA((1,)),
        ],
    )
    rows_b = call(
        functools.partial(pick_kernel, groups),
        shape((groups * SLOTS, width), bf16),
        (asked, staged),
        8 * MIB,
        50_000_000_000,
        1_000_000_000,
    )
    weights = (entry_weights, down_weights, saved_projections)
    packs = (
        shape((width, 6 * half), bf16),
        shape((6 * half, width), bf16),
        shape((chips * PAIR, 4 * half), f32),
    )
    packed = call(
        functools.partial(pack_own_kernel, chips, direct),
        packs,
        (),
        8 * MIB,
        10_000_000,
        5_000_000,
        after=(rows_b,),
        far=weights,
        scratch=[
            *[pltpu.VMEM(value.shape, value.dtype) for value in weights],
            pltpu.SemaphoreType.DMA((len(weights),)),
        ],
    )
    rows_b = along_sections(rows_b, -1)
    weights = [across_owners(value, 1) for value in weights]
    message, whole = call(
        functools.partial(merge_kernel, groups),
        (shape((groups, PAIR, width), bf16), block),
        (layer_input, pick_x, rows_b, send_scale, staged),
        8 * MIB,
        100_000,
        100_000,
        after=(*packed, *weights),
    )
    upstream = along_sections(whole, -1)
    if direct:
        arrived = [message[0]] + [across_owners(message[0], CORES * flip) for flip in range(1, chips)]
    else:
        same_core = [list(range(core, owners, CORES)) for core in range(CORES)]
        spread = jnp.repeat(message, chips // groups, axis=0)
        gathered = lax.all_to_all(
            spread, "expert", 0, 0, axis_index_groups=same_core, tiled=True
        )
        arrived = [gathered[index] for index in range(chips)]
    packed = call(
        functools.partial(pack_pair_kernel, chips, direct),
        packs,
        (*weights, *packed),
        8 * MIB,
        10_000_000,
        5_000_000,
        after=(arrived[-1],),
        aliases={3: 0, 4: 1, 5: 2},
    )
    results = call(
        functools.partial(expert_kernel, chips),
        (shape((PAIR, width), bf16),) * chips,
        (*arrived, *packed),
        16 * MIB,
        800_000_000,
        5_000_000,
    )
    if direct:
        returned = [results[0]] + [
            across_owners(results[flip], CORES * flip) for flip in range(1, chips)
        ]
    else:
        gathered = lax.all_to_all(
            jnp.stack(results), "expert", 0, 0, axis_index_groups=same_core, tiled=True
        )
        returned = [gathered[index] for index in range(chips)]
    return call(
        functools.partial(finish_kernel, groups, chips),
        (block, block),
        (layer_input, upstream, place_x, place_u, sum_scale, *returned),
        16 * MIB,
        10_000_000,
        1_000_000,
    )


def solution(mesh):
    rows = P("segment", "expert", None)
    blocks = P("segment", "expert", None, None)
    return jax.shard_map(
        shards,
        mesh=mesh,
        in_specs=(rows,) * 6 + (blocks,) * 3,
        out_specs=(rows, rows),
        check_vma=False,
    )
```

```python
import functools

import jax
import jax.numpy as jnp
from jax import lax
from jax.experimental import pallas as pl
from jax.experimental.pallas import tpu as pltpu
from jax.sharding import PartitionSpec as P

FSPLIT = 8
CAP = 5
CORES = 2
SLOTS = 8
PAIR = 2 * SLOTS
MIB = 1 << 20


def along_sections(value, steps):
    count = lax.axis_size("segment")
    pairs = [(source, (source + steps) % count) for source in range(count)]
    return lax.ppermute(value, "segment", pairs)


def across_owners(value, flip):
    count = lax.axis_size("expert")
    return lax.ppermute(value, "expert", [(source, source ^ flip) for source in range(count)])


def call(kernel, outs, args, limit, flops, moved, after=(), aliases=None, far=(), scratch=()):
    whole = pl.BlockSpec(memory_space=pltpu.VMEM)
    anywhere = pl.BlockSpec(memory_space=pl.ANY)
    distant = pl.BlockSpec(memory_space=pltpu.HBM)
    waits = len(after)

    def body(*refs):
        kernel(*refs[waits:])

    return pl.pallas_call(
        body,
        out_shape=outs,
        in_specs=[anywhere] * waits + [distant] * len(far) + [whole] * len(args),
        out_specs=jax.tree.map(lambda _: whole, outs),
        scratch_shapes=scratch,
        input_output_aliases={
            waits + len(far) + key: value for key, value in (aliases or {}).items()
        },
        compiler_params=pltpu.CompilerParams(vmem_limit_bytes=limit),
        cost_estimate=pl.CostEstimate(flops=flops, bytes_accessed=moved, transcendentals=0),
    )(*after, *[pltpu.with_memory_space_constraint(value, pltpu.HBM) for value in far], *args)


def dot(left, right):
    return jnp.dot(left, right, preferred_element_type=jnp.float32)


def hits(routes, group):
    return jnp.where(routes == group, 1.0, 0.0)


def slot_picks(routes, group, rows, offset):
    toks = routes.shape[1]
    shape = (toks, toks)
    before = lax.broadcasted_iota(jnp.int32, shape, 0) < lax.broadcasted_iota(jnp.int32, shape, 1)
    before = jnp.where(before, 1.0, 0.0).astype(jnp.bfloat16)
    along = jnp.sum(hits(routes, group), axis=0, keepdims=True)
    along = jnp.broadcast_to(along, (rows, toks))
    rank = dot(along.astype(jnp.bfloat16), before)
    slot = lax.broadcasted_iota(jnp.int32, (rows, toks), 0) - offset
    return jnp.where(rank == slot.astype(jnp.float32), along, 0.0)


def fetch(sources, targets, semaphores):
    copies = [
        pltpu.make_async_copy(source, target, semaphores.at[index])
        for index, (source, target) in enumerate(zip(sources, targets))
    ]
    for copy in copies:
        copy.start()
    for copy in copies:
        copy.wait()


def pick_kernel(groups, routes, staged, rows):
    picks = [slot_picks(routes[0], group, SLOTS, 0) for group in range(groups)]
    picks = picks[0] if groups == 1 else jnp.concatenate(picks, axis=0)
    rows[...] = dot(picks.astype(jnp.bfloat16), staged[0]).astype(jnp.bfloat16)


def release_kernel(staged, whole):
    whole[...] = staged[...]


def merge_kernel(groups, x, pick_x, rows_b, send_scale, message):
    all_a = dot(pick_x[...], x[0])
    all_b = rows_b[...].astype(jnp.float32)
    for group in range(groups):
        one = slice(group * SLOTS, (group + 1) * SLOTS)
        scaled = all_b[one] * send_scale[pl.ds(group * SLOTS, SLOTS), :1]
        both = [all_a[group * PAIR : group * PAIR + SLOTS], scaled]
        message[group] = jnp.concatenate(both, axis=0).astype(jnp.bfloat16)


def prepare_kernel(groups, *refs):
    far, refs = refs[:5], refs[5:]
    staged, pick_x, place_x, place_u, send_scale, sum_scale = refs[:6]
    near, semaphores, stage_semaphore = refs[6:10], refs[10], refs[11]
    stage = pltpu.make_async_copy(far[4], staged, stage_semaphore.at[0])
    stage.start()
    fetch(far[:4], near, semaphores)
    routes_a, logits_a, routes_b, logits_b = near

    def micro(routes, logits, offset):
        scores = jnp.exp(logits[0])
        probs = scores / jnp.sum(scores, axis=0, keepdims=True)
        picks, scales = [], []
        for group in range(groups):
            pick = slot_picks(routes[0], group, PAIR, offset)
            prob = jnp.sum(hits(routes[0], group) * probs, axis=0, keepdims=True)
            scales.append(jnp.sum(pick * prob, axis=1, keepdims=True))
            picks.append(pick)
        return picks, scales

    picks_a, scales_a = micro(routes_a, logits_a, 0)
    picks_b, scales_b = micro(routes_b, logits_b, SLOTS)
    place_x[...] = jnp.concatenate(picks_a * 3, axis=0).T.astype(jnp.bfloat16)
    place_u[...] = jnp.concatenate(picks_b * 3, axis=0).T.astype(jnp.bfloat16)
    half_row = lax.broadcasted_iota(jnp.int32, (PAIR, 128), 0)
    for group in range(groups):
        rows = pl.ds(group * PAIR, PAIR)
        pick_x[rows, :] = picks_a[group].astype(jnp.bfloat16)
        send_scale[pl.ds(group * SLOTS, SLOTS), :] = jnp.broadcast_to(
            scales_b[group][SLOTS:], (SLOTS, 128)
        )
        sum_scale[rows, :] = jnp.where(half_row < SLOTS, scales_a[group], 1.0)
    stage.wait()


def pack_half(index, chips, mixed, entry, down, saved, lower, second, factors):
    half = down.shape[2]
    gate = slice(index * half, (index + 1) * half)
    upper = slice((2 + index) * half, (3 + index) * half)
    lower[:, gate] = down[0, 0].T
    turned = entry[0, 0].T
    second[gate, :] = turned[:half]
    second[upper, :] = turned[half:]

    me = lax.axis_index("expert")
    held = saved.shape[2]
    shape = (chips * PAIR, held)
    line = lax.broadcasted_iota(jnp.int32, shape, 0)
    origin = line // PAIR
    if mixed:
        origin = origin ^ (me // CORES)
    slot = line % PAIR - SLOTS
    wanted = (CORES * origin + me % CORES) * CAP + slot
    wanted = jnp.where((slot >= 0) & (slot < CAP), wanted, -1)
    chosen = jnp.where(wanted == lax.broadcasted_iota(jnp.int32, shape, 1), 1.0, 0.0)
    stored = dot(chosen.astype(jnp.bfloat16), saved[0, 0])
    gates = stored[:, :half]
    uppers = stored[:, half:]
    logistic = jax.nn.sigmoid(gates)
    factors[:, gate] = uppers * logistic * (1.0 + gates * (1.0 - logistic))
    factors[:, upper] = gates * logistic


def pack_own_kernel(chips, mixed, *refs):
    entry_far, down_far, saved_far, entry, down, lower, second, factors, saved, semaphores = refs
    half = down.shape[2]
    rows = second.at[pl.ds(4 * half, half)]
    fetch(
        (entry_far, down_far, saved_far, down_far.at[0, 0]),
        (entry, down, saved, rows),
        semaphores,
    )
    pack_half(0, chips, mixed, entry, down, saved, lower, second, factors)


def pack_pair_kernel(chips, mixed, entry, down, saved, *refs):
    lower, second, factors = refs[3:]
    half = down.shape[2]
    second[5 * half :, :] = down[0, 0]
    pack_half(1, chips, mixed, entry, down, saved, lower, second, factors)


def expert_kernel(chips, *refs):
    arrived = refs[:chips]
    entries = refs[chips : chips + 2]
    lower, second, factors = refs[chips + 2 : chips + 5]
    results = refs[chips + 5 :]
    rows = jnp.concatenate([ref[...] for ref in arrived], axis=0)
    back = dot(rows, lower[...])
    half = back.shape[1] // 2
    grads = jnp.concatenate([back, back], axis=1) * factors[...]
    hidden = []
    for entry in entries:
        made = dot(rows, entry[0, 0])
        gate = made[:, :half]
        hidden.append(gate * jax.nn.sigmoid(gate) * made[:, half:])
    hidden = jnp.concatenate(hidden, axis=1)
    line = lax.broadcasted_iota(jnp.int32, hidden.shape, 0) % PAIR
    hidden = jnp.where(line < SLOTS, hidden, 0.0)
    inner = jnp.concatenate([grads.astype(jnp.bfloat16), hidden.astype(jnp.bfloat16)], axis=1)
    total = dot(inner, second[...]).astype(jnp.bfloat16)
    for index, ref in enumerate(results):
        ref[...] = total[index * PAIR : (index + 1) * PAIR]


def finish_kernel(groups, chips, *refs):
    x, u, place_x, place_u, sum_scale = refs[:5]
    returned = refs[5 : 5 + chips][::-1]
    out_x, out_u = refs[5 + chips :]
    share = chips // groups
    sums = []
    for group in range(groups):
        total = returned[group * share][...].astype(jnp.float32)
        for ref in returned[group * share + 1 : (group + 1) * share]:
            total = total + ref[...].astype(jnp.float32)
        sums.append(total * sum_scale[pl.ds(group * PAIR, PAIR), :1])
    rest = sums[0] if groups == 1 else jnp.concatenate(sums, axis=0)
    pieces = []
    for _ in range(3):
        piece = rest.astype(jnp.bfloat16)
        pieces.append(piece)
        rest = rest - piece.astype(jnp.float32)
    pieces = jnp.concatenate(pieces, axis=0)
    out_x[0] = (x[0].astype(jnp.float32) + dot(place_x[...], pieces)).astype(jnp.bfloat16)
    out_u[0] = (u[0].astype(jnp.float32) + dot(place_u[...], pieces)).astype(jnp.bfloat16)


def shards(
    section_output,
    section_gradient,
    forward_routes,
    forward_logits,
    backward_routes,
    backward_logits,
    entry_weights,
    down_weights,
    saved_projections,
):
    owners = lax.axis_size("expert")
    groups = owners // FSPLIT
    chips = owners // CORES
    direct = chips == 4
    toks, width = section_output.shape[1:]
    half = down_weights.shape[2]
    shape = jax.ShapeDtypeStruct
    bf16, f32 = jnp.bfloat16, jnp.float32
    routes_a, logits_a, routes_b, logits_b = [
        jnp.swapaxes(value, 1, 2)
        for value in (forward_routes, forward_logits, backward_routes, backward_logits)
    ]

    block = shape((1, toks, width), bf16)
    asked = along_sections(routes_b, 1)
    layer_input = along_sections(section_output, 1)
    own_values = (routes_a, logits_a, routes_b, logits_b)
    staged, pick_x, place_x, place_u, send_scale, sum_scale = call(
        functools.partial(prepare_kernel, groups),
        (
            block,
            shape((groups * PAIR, toks), bf16),
            shape((toks, 3 * groups * PAIR), bf16),
            shape((toks, 3 * groups * PAIR), bf16),
            shape((groups * SLOTS, 128), f32),
            shape((groups * PAIR, 128), f32),
        ),
        (),
        8 * MIB,
        10_000_000,
        1_000_000,
        far=(*own_values, section_gradient),
        scratch=[
            *[pltpu.VMEM(value.shape, value.dtype) for value in own_values],
            pltpu.SemaphoreType.DMA((len(own_values),)),
            pltpu.SemaphoreType.DMA((1,)),
        ],
    )
    rows_b = call(
        functools.partial(pick_kernel, groups),
        shape((groups * SLOTS, width), bf16),
        (asked, staged),
        8 * MIB,
        10_000_000_000,
        1_000_000_000,
    )
    weights = (entry_weights, down_weights, saved_projections)
    packs = (
        shape((width, 2 * half), bf16),
        shape((6 * half, width), bf16),
        shape((chips * PAIR, 4 * half), f32),
    )
    entry_own, down_own, *packed = call(
        functools.partial(pack_own_kernel, chips, direct),
        (shape(entry_weights.shape, bf16), shape(down_weights.shape, bf16), *packs),
        (),
        8 * MIB,
        10_000_000,
        5_000_000,
        after=(rows_b,),
        far=weights,
        scratch=[
            pltpu.VMEM(saved_projections.shape, bf16),
            pltpu.SemaphoreType.DMA((len(weights) + 1,)),
        ],
    )
    rows_b = along_sections(rows_b, -1)
    weights = [across_owners(value, 1) for value in (entry_own, down_own, saved_projections)]
    message = call(
        functools.partial(merge_kernel, groups),
        shape((groups, PAIR, width), bf16),
        (layer_input, pick_x, rows_b, send_scale),
        8 * MIB,
        50_000_000_000,
        100_000,
        after=(*packed, weights[2]),
    )
    whole = call(
        release_kernel,
        block,
        (staged,),
        8 * MIB,
        1,
        1,
        after=(message, *weights[:2]),
    )
    upstream = along_sections(whole, -1)
    if direct:
        arrived = [message[0]] + [across_owners(message[0], CORES * flip) for flip in range(1, chips)]
    else:
        same_core = [list(range(core, owners, CORES)) for core in range(CORES)]
        spread = jnp.repeat(message, chips // groups, axis=0)
        gathered = lax.all_to_all(
            spread, "expert", 0, 0, axis_index_groups=same_core, tiled=True
        )
        arrived = [gathered[index] for index in range(chips)]
    packed = call(
        functools.partial(pack_pair_kernel, chips, direct),
        packs,
        (*weights, *packed),
        8 * MIB,
        10_000_000_000,
        5_000_000,
        after=(arrived[-1],),
        aliases={3: 0, 4: 1, 5: 2},
    )
    results = call(
        functools.partial(expert_kernel, chips),
        (shape((PAIR, width), bf16),) * chips,
        (*arrived, entry_own, weights[0], *packed),
        16 * MIB,
        800_000_000,
        5_000_000,
    )
    if direct:
        returned = [results[0]] + [
            across_owners(results[flip], CORES * flip) for flip in range(1, chips)
        ]
    else:
        gathered = lax.all_to_all(
            jnp.stack(results), "expert", 0, 0, axis_index_groups=same_core, tiled=True
        )
        returned = [gathered[index] for index in range(chips)]
    return call(
        functools.partial(finish_kernel, groups, chips),
        (block, block),
        (layer_input, upstream, place_x, place_u, sum_scale, *returned[::-1]),
        16 * MIB,
        10_000_000,
        1_000_000,
    )


def solution(mesh):
    rows = P("segment", "expert", None)
    blocks = P("segment", "expert", None, None)
    return jax.shard_map(
        shards,
        mesh=mesh,
        in_specs=(rows,) * 6 + (blocks,) * 3,
        out_specs=(rows, rows),
        check_vma=False,
    )
```

```python
import functools

import jax
import jax.numpy as jnp
from jax import lax
from jax.experimental import pallas as pl
from jax.experimental.pallas import tpu as pltpu
from jax.sharding import PartitionSpec as P

FSPLIT = 8
CAP = 5
CORES = 2
ROWS = 16
LINES = 8
FEW = 2 * CAP - LINES
PARTS = LINES // FEW
MIB = 1 << 20


def along_sections(value, steps):
    count = lax.axis_size("segment")
    pairs = [(source, (source + steps) % count) for source in range(count)]
    return lax.ppermute(value, "segment", pairs)


def across_owners(value, flip):
    count = lax.axis_size("expert")
    return lax.ppermute(value, "expert", [(source, source ^ flip) for source in range(count)])


def call(kernel, outs, args, limit, flops, moved, after=(), aliases=None, far=(), scratch=()):
    whole = pl.BlockSpec(memory_space=pltpu.VMEM)
    anywhere = pl.BlockSpec(memory_space=pl.ANY)
    distant = pl.BlockSpec(memory_space=pltpu.HBM)
    waits = len(after)

    def body(*refs):
        kernel(*refs[waits:])

    return pl.pallas_call(
        body,
        out_shape=outs,
        in_specs=[anywhere] * waits + [distant] * len(far) + [whole] * len(args),
        out_specs=jax.tree.map(lambda _: whole, outs),
        scratch_shapes=scratch,
        input_output_aliases={
            waits + len(far) + key: value for key, value in (aliases or {}).items()
        },
        compiler_params=pltpu.CompilerParams(vmem_limit_bytes=limit),
        cost_estimate=pl.CostEstimate(flops=flops, bytes_accessed=moved, transcendentals=0),
    )(*after, *[pltpu.with_memory_space_constraint(value, pltpu.HBM) for value in far], *args)


def dot(left, right):
    return jnp.dot(left, right, preferred_element_type=jnp.float32)


def hits(routes, group):
    return jnp.where(routes == group, 1.0, 0.0)


def slot_picks(routes, group, slot):
    rows, toks = slot.shape
    shape = (toks, toks)
    before = lax.broadcasted_iota(jnp.int32, shape, 0) < lax.broadcasted_iota(jnp.int32, shape, 1)
    before = jnp.where(before, 1.0, 0.0).astype(jnp.bfloat16)
    along = jnp.sum(hits(routes, group), axis=0, keepdims=True)
    along = jnp.broadcast_to(along, (rows, toks))
    rank = dot(along.astype(jnp.bfloat16), before)
    return jnp.where(rank == slot.astype(jnp.float32), along, 0.0)


def fold(first, few):
    part = few.shape[1] // PARTS
    few = [few[:, index * part : (index + 1) * part] for index in range(PARTS)]
    return jnp.concatenate([first, jnp.concatenate(few, axis=0)], axis=1)


def unfold(message):
    width = message.shape[1] * PARTS // (PARTS + 1)
    few = [message[index * FEW : (index + 1) * FEW, width:] for index in range(PARTS)]
    return message[:, :width], jnp.concatenate(few, axis=1)


def fetch(sources, targets, semaphores):
    copies = [
        pltpu.make_async_copy(source, target, semaphores.at[index])
        for index, (source, target) in enumerate(zip(sources, targets))
    ]
    for copy in copies:
        copy.start()
    for copy in copies:
        copy.wait()


def pick_kernel(groups, routes, staged, rows):
    row = lax.broadcasted_iota(jnp.int32, (LINES, staged.shape[1]), 0)
    slot = jnp.where(row < FEW, CAP - FEW + row, row - CAP)
    picks = [slot_picks(routes[0], group, slot) for group in range(groups)]
    picks = picks[0] if groups == 1 else jnp.concatenate(picks, axis=0)
    rows[...] = dot(picks.astype(jnp.bfloat16), staged[0]).astype(jnp.bfloat16)


def release_kernel(staged, whole):
    whole[...] = staged[...]


def merge_kernel(groups, x, pick_x, rows_b, message):
    all_a = dot(pick_x[...], x[0])
    all_b = rows_b[...].astype(jnp.float32)
    for group in range(groups):
        rows = slice(group * LINES, (group + 1) * LINES)
        b = all_b[rows]
        line = lax.broadcasted_iota(jnp.int32, b.shape, 0)
        first = jnp.where(line < CAP, all_a[rows], b)
        message[group] = fold(first, b[:FEW]).astype(jnp.bfloat16)


def prepare_kernel(groups, *refs):
    far, refs = refs[:5], refs[5:]
    staged, pick_x, place_x, place_u, sum_scale = refs[:5]
    near, semaphores, stage_semaphore = refs[5:9], refs[9], refs[10]
    stage = pltpu.make_async_copy(far[4], staged, stage_semaphore.at[0])
    stage.start()
    fetch(far[:4], near, semaphores)
    routes_a, logits_a, routes_b, logits_b = near

    def micro(routes, logits, offset):
        scores = jnp.exp(logits[0])
        probs = scores / jnp.sum(scores, axis=0, keepdims=True)
        slot = lax.broadcasted_iota(jnp.int32, (ROWS, routes.shape[2]), 0) - offset
        picks, scales = [], []
        for group in range(groups):
            pick = slot_picks(routes[0], group, slot)
            prob = jnp.sum(hits(routes[0], group) * probs, axis=0, keepdims=True)
            scales.append(jnp.sum(pick * prob, axis=1, keepdims=True))
            picks.append(pick)
        return picks, scales

    picks_a, scales_a = micro(routes_a, logits_a, 0)
    picks_b, scales_b = micro(routes_b, logits_b, CAP)
    place_x[...] = jnp.concatenate(picks_a * 3, axis=0).T.astype(jnp.bfloat16)
    place_u[...] = jnp.concatenate(picks_b * 3, axis=0).T.astype(jnp.bfloat16)
    first = [pick[:LINES] for pick in picks_a]
    pick_x[...] = (first[0] if groups == 1 else jnp.concatenate(first, axis=0)).astype(jnp.bfloat16)
    for group in range(groups):
        scale = scales_a[group] + scales_b[group]
        sum_scale[pl.ds(group * ROWS, ROWS), :] = jnp.broadcast_to(scale, (ROWS, 128))
    stage.wait()


def lines_of(shape, chips):
    line = lax.broadcasted_iota(jnp.int32, shape, 0)
    early = line < chips * LINES
    late = line - chips * LINES
    origin = jnp.where(early, line // LINES, late // FEW)
    slot = jnp.where(early, line % LINES - CAP, CAP - FEW + late % FEW)
    return origin, slot


def pack_half(index, chips, mixed, entry, down, saved, lower, second, factors):
    half = down.shape[2]
    gate = slice(index * half, (index + 1) * half)
    upper = slice((2 + index) * half, (3 + index) * half)
    lower[:, gate] = down[0, 0].T
    turned = entry[0, 0].T
    second[gate, :] = turned[:half]
    second[upper, :] = turned[half:]

    me = lax.axis_index("expert")
    held = saved.shape[2]
    shape = (factors.shape[0], held)
    origin, slot = lines_of(shape, chips)
    if mixed:
        origin = origin ^ (me // CORES)
    wanted = (CORES * origin + me % CORES) * CAP + slot
    wanted = jnp.where(slot >= 0, wanted, -1)
    chosen = jnp.where(wanted == lax.broadcasted_iota(jnp.int32, shape, 1), 1.0, 0.0)
    stored = dot(chosen.astype(jnp.bfloat16), saved[0, 0])
    gates = stored[:, :half]
    uppers = stored[:, half:]
    logistic = jax.nn.sigmoid(gates)
    factors[:, gate] = uppers * logistic * (1.0 + gates * (1.0 - logistic))
    factors[:, upper] = gates * logistic


def pack_own_kernel(chips, mixed, *refs):
    entry_far, down_far, saved_far, entry, down, lower, second, factors, saved, semaphores = refs
    half = down.shape[2]
    rows = second.at[pl.ds(4 * half, half)]
    fetch(
        (entry_far, down_far, saved_far, down_far.at[0, 0]),
        (entry, down, saved, rows),
        semaphores,
    )
    pack_half(0, chips, mixed, entry, down, saved, lower, second, factors)


def pack_pair_kernel(chips, mixed, entry, down, saved, *refs):
    lower, second, factors = refs[3:]
    half = down.shape[2]
    second[5 * half :, :] = down[0, 0]
    pack_half(1, chips, mixed, entry, down, saved, lower, second, factors)


def expert_kernel(chips, *refs):
    arrived = refs[:chips]
    entries = refs[chips : chips + 2]
    lower, second, factors = refs[chips + 2 : chips + 5]
    results = refs[chips + 5 :]
    firsts, fews = zip(*[unfold(ref[...].astype(jnp.float32)) for ref in arrived])
    rows = jnp.concatenate([*firsts, *fews], axis=0).astype(jnp.bfloat16)
    back = dot(rows, lower[...])
    half = back.shape[1] // 2
    grads = jnp.concatenate([back, back], axis=1) * factors[...]
    hidden = []
    for entry in entries:
        made = dot(rows, entry[0, 0])
        gate = made[:, :half]
        hidden.append(gate * jax.nn.sigmoid(gate) * made[:, half:])
    hidden = jnp.concatenate(hidden, axis=1)
    _, slot = lines_of(hidden.shape, chips)
    hidden = jnp.where(slot < 0, hidden, 0.0)
    inner = jnp.concatenate([grads.astype(jnp.bfloat16), hidden.astype(jnp.bfloat16)], axis=1)
    total = dot(inner, second[...])
    for index, ref in enumerate(results):
        late = chips * LINES + index * FEW
        first = total[index * LINES : (index + 1) * LINES]
        ref[...] = fold(first, total[late : late + FEW]).astype(jnp.bfloat16)


def finish_kernel(groups, chips, *refs):
    x, u, place_x, place_u, sum_scale = refs[:5]
    returned = refs[5 : 5 + chips][::-1]
    out_x, out_u = refs[5 + chips :]
    share = chips // groups
    sums = []
    for group in range(groups):
        total = returned[group * share][...].astype(jnp.float32)
        for ref in returned[group * share + 1 : (group + 1) * share]:
            total = total + ref[...].astype(jnp.float32)
        first, few = unfold(total)
        empty = jnp.zeros((ROWS - 2 * CAP, first.shape[1]), jnp.float32)
        total = jnp.concatenate([first, few, empty], axis=0)
        sums.append(total * sum_scale[pl.ds(group * ROWS, ROWS), :1])
    rest = sums[0] if groups == 1 else jnp.concatenate(sums, axis=0)
    pieces = []
    for _ in range(3):
        piece = rest.astype(jnp.bfloat16)
        pieces.append(piece)
        rest = rest - piece.astype(jnp.float32)
    pieces = jnp.concatenate(pieces, axis=0)
    out_x[0] = (x[0].astype(jnp.float32) + dot(place_x[...], pieces)).astype(jnp.bfloat16)
    out_u[0] = (u[0].astype(jnp.float32) + dot(place_u[...], pieces)).astype(jnp.bfloat16)


def shards(
    section_output,
    section_gradient,
    forward_routes,
    forward_logits,
    backward_routes,
    backward_logits,
    entry_weights,
    down_weights,
    saved_projections,
):
    owners = lax.axis_size("expert")
    groups = owners // FSPLIT
    chips = owners // CORES
    direct = chips == 4
    toks, width = section_output.shape[1:]
    half = down_weights.shape[2]
    shape = jax.ShapeDtypeStruct
    bf16, f32 = jnp.bfloat16, jnp.float32
    routes_a, logits_a, routes_b, logits_b = [
        jnp.swapaxes(value, 1, 2)
        for value in (forward_routes, forward_logits, backward_routes, backward_logits)
    ]

    block = shape((1, toks, width), bf16)
    folded = (LINES, width + width // PARTS)
    asked = along_sections(routes_b, 1)
    layer_input = along_sections(section_output, 1)
    own_values = (routes_a, logits_a, routes_b, logits_b)
    staged, pick_x, place_x, place_u, sum_scale = call(
        functools.partial(prepare_kernel, groups),
        (
            block,
            shape((groups * LINES, toks), bf16),
            shape((toks, 3 * groups * ROWS), bf16),
            shape((toks, 3 * groups * ROWS), bf16),
            shape((groups * ROWS, 128), f32),
        ),
        (),
        8 * MIB,
        10_000_000,
        1_000_000,
        far=(*own_values, section_gradient),
        scratch=[
            *[pltpu.VMEM(value.shape, value.dtype) for value in own_values],
            pltpu.SemaphoreType.DMA((len(own_values),)),
            pltpu.SemaphoreType.DMA((1,)),
        ],
    )
    rows_b = call(
        functools.partial(pick_kernel, groups),
        shape((groups * LINES, width), bf16),
        (asked, staged),
        8 * MIB,
        10_000_000_000,
        1_000_000_000,
    )
    weights = (entry_weights, down_weights, saved_projections)
    packs = (
        shape((width, 2 * half), bf16),
        shape((6 * half, width), bf16),
        shape((2 * CAP * chips, 4 * half), f32),
    )
    entry_own, down_own, *packed = call(
        functools.partial(pack_own_kernel, chips, direct),
        (shape(entry_weights.shape, bf16), shape(down_weights.shape, bf16), *packs),
        (),
        8 * MIB,
        10_000_000,
        5_000_000,
        after=(rows_b,),
        far=weights,
        scratch=[
            pltpu.VMEM(saved_projections.shape, bf16),
            pltpu.SemaphoreType.DMA((len(weights) + 1,)),
        ],
    )
    rows_b = along_sections(rows_b, -1)
    weights = [across_owners(value, 1) for value in (entry_own, down_own, saved_projections)]
    message = call(
        functools.partial(merge_kernel, groups),
        shape((groups, *folded), bf16),
        (layer_input, pick_x, rows_b),
        8 * MIB,
        50_000_000_000,
        100_000,
        after=(*packed, weights[2]),
    )
    whole = call(
        release_kernel,
        block,
        (staged,),
        8 * MIB,
        1,
        1,
        after=(message, *weights[:2]),
    )
    upstream = along_sections(whole, -1)
    if direct:
        arrived = [message[0]] + [across_owners(message[0], CORES * flip) for flip in range(1, chips)]
    else:
        same_core = [list(range(core, owners, CORES)) for core in range(CORES)]
        spread = jnp.repeat(message, chips // groups, axis=0)
        gathered = lax.all_to_all(
            spread, "expert", 0, 0, axis_index_groups=same_core, tiled=True
        )
        arrived = [gathered[index] for index in range(chips)]
    packed = call(
        functools.partial(pack_pair_kernel, chips, direct),
        packs,
        (*weights, *packed),
        8 * MIB,
        10_000_000_000,
        5_000_000,
        after=(arrived[-1],),
        aliases={3: 0, 4: 1, 5: 2},
    )
    results = call(
        functools.partial(expert_kernel, chips),
        (shape(folded, bf16),) * chips,
        (*arrived, entry_own, weights[0], *packed),
        16 * MIB,
        800_000_000,
        5_000_000,
    )
    if direct:
        returned = [results[0]] + [
            across_owners(results[flip], CORES * flip) for flip in range(1, chips)
        ]
    else:
        gathered = lax.all_to_all(
            jnp.stack(results), "expert", 0, 0, axis_index_groups=same_core, tiled=True
        )
        returned = [gathered[index] for index in range(chips)]
    return call(
        functools.partial(finish_kernel, groups, chips),
        (block, block),
        (layer_input, upstream, place_x, place_u, sum_scale, *returned[::-1]),
        16 * MIB,
        10_000_000,
        1_000_000,
    )


def solution(mesh):
    rows = P("segment", "expert", None)
    blocks = P("segment", "expert", None, None)
    return jax.shard_map(
        shards,
        mesh=mesh,
        in_specs=(rows,) * 6 + (blocks,) * 3,
        out_specs=(rows, rows),
        check_vma=False,
    )
```

```python
import functools

import jax
import jax.numpy as jnp
from jax import lax
from jax.experimental import pallas as pl
from jax.experimental.pallas import tpu as pltpu
from jax.sharding import PartitionSpec as P

FSPLIT = 8
CAP = 5
CORES = 2
ROWS = 16
LINES = 8
FEW = 2 * CAP - LINES
PARTS = LINES // FEW
MIB = 1 << 20


def along_sections(value, steps):
    count = lax.axis_size("segment")
    pairs = [(source, (source + steps) % count) for source in range(count)]
    return lax.ppermute(value, "segment", pairs)


def across_owners(value, flip):
    count = lax.axis_size("expert")
    return lax.ppermute(value, "expert", [(source, source ^ flip) for source in range(count)])


def call(kernel, outs, args, limit, flops, moved, after=(), aliases=None, far=(), scratch=()):
    whole = pl.BlockSpec(memory_space=pltpu.VMEM)
    anywhere = pl.BlockSpec(memory_space=pl.ANY)
    distant = pl.BlockSpec(memory_space=pltpu.HBM)
    waits = len(after)

    def body(*refs):
        kernel(*refs[waits:])

    return pl.pallas_call(
        body,
        out_shape=outs,
        in_specs=[anywhere] * waits + [distant] * len(far) + [whole] * len(args),
        out_specs=jax.tree.map(lambda _: whole, outs),
        scratch_shapes=scratch,
        input_output_aliases={
            waits + len(far) + key: value for key, value in (aliases or {}).items()
        },
        compiler_params=pltpu.CompilerParams(vmem_limit_bytes=limit),
        cost_estimate=pl.CostEstimate(flops=flops, bytes_accessed=moved, transcendentals=0),
    )(*after, *[pltpu.with_memory_space_constraint(value, pltpu.HBM) for value in far], *args)


def dot(left, right):
    return jnp.dot(left, right, preferred_element_type=jnp.float32)


def dot_by_columns(left, right):
    spans = range(0, right.shape[1], 128)
    return jnp.concatenate([dot(left, right[:, start : start + 128]) for start in spans], axis=1)


def hits(routes, group):
    return jnp.where(routes == group, 1.0, 0.0)


def slot_picks(routes, group, slot):
    rows, toks = slot.shape
    shape = (toks, toks)
    before = lax.broadcasted_iota(jnp.int32, shape, 0) < lax.broadcasted_iota(jnp.int32, shape, 1)
    before = jnp.where(before, 1.0, 0.0).astype(jnp.bfloat16)
    along = jnp.sum(hits(routes, group), axis=0, keepdims=True)
    along = jnp.broadcast_to(along, (rows, toks))
    rank = dot(along.astype(jnp.bfloat16), before)
    return jnp.where(rank == slot.astype(jnp.float32), along, 0.0)


def fold(first, few):
    part = few.shape[1] // PARTS
    few = [few[:, index * part : (index + 1) * part] for index in range(PARTS)]
    return jnp.concatenate([first, jnp.concatenate(few, axis=0)], axis=1)


def runs(width):
    line_width = width * CAP // LINES
    rest = width - line_width
    place, found = 0, []
    while place < CAP * rest:
        row, column = divmod(place, rest)
        line, start = divmod(place, line_width)
        length = min(rest - column, line_width - start)
        found.append((row, line_width + column, CAP + line, start, length))
        place += length
    return line_width, found


def fold_rows(rows):
    line_width, found = runs(rows.shape[1])
    lines = [[] for _ in range(LINES - CAP)]
    for row, column, line, _, length in found:
        lines[line - CAP].append(rows[row : row + 1, column : column + length])
    lines = [jnp.concatenate(parts, axis=1) for parts in lines]
    return jnp.concatenate([rows[:CAP, :line_width], *lines], axis=0)


def unfold_rows(lines, width):
    line_width, found = runs(width)
    rows = [[lines[row : row + 1]] for row in range(CAP)]
    for row, _, line, start, length in found:
        rows[row].append(lines[line : line + 1, start : start + length])
    return jnp.concatenate([jnp.concatenate(parts, axis=1) for parts in rows], axis=0)


def unfold(message):
    width = message.shape[1] * PARTS // (PARTS + 1)
    few = [message[index * FEW : (index + 1) * FEW, width:] for index in range(PARTS)]
    return message[:, :width], jnp.concatenate(few, axis=1)


def fetch(sources, targets, semaphores):
    copies = [
        pltpu.make_async_copy(source, target, semaphores.at[index])
        for index, (source, target) in enumerate(zip(sources, targets))
    ]
    for copy in copies:
        copy.start()
    for copy in copies:
        copy.wait()


def pick_kernel(groups, routes, staged, rows):
    slot = lax.broadcasted_iota(jnp.int32, (LINES, staged.shape[1]), 0)
    for group in range(groups):
        pick = slot_picks(routes[0], group, slot).astype(jnp.bfloat16)
        rows[group] = fold_rows(dot(pick, staged[0])).astype(jnp.bfloat16)


def release_kernel(staged, whole):
    whole[...] = staged[...]


def merge_kernel(groups, x, pick_x, rows_b, message):
    all_a = dot(pick_x[...], x[0])
    for group in range(groups):
        a = all_a[group * LINES : group * LINES + CAP]
        b = unfold_rows(rows_b[group].astype(jnp.float32), x.shape[2])
        first = jnp.concatenate([a, b[: CAP - FEW]], axis=0)
        message[group] = fold(first, b[CAP - FEW :]).astype(jnp.bfloat16)


def prepare_kernel(groups, *refs):
    far, refs = refs[:5], refs[5:]
    staged, pick_x, place_x, place_u, sum_scale = refs[:5]
    near, semaphores, stage_semaphore = refs[5:9], refs[9], refs[10]
    stage = pltpu.make_async_copy(far[4], staged, stage_semaphore.at[0])
    stage.start()
    fetch(far[:4], near, semaphores)
    routes_a, logits_a, routes_b, logits_b = near

    def micro(routes, logits, offset):
        scores = jnp.exp(logits[0])
        probs = scores / jnp.sum(scores, axis=0, keepdims=True)
        slot = lax.broadcasted_iota(jnp.int32, (ROWS, routes.shape[2]), 0) - offset
        picks, scales = [], []
        for group in range(groups):
            pick = slot_picks(routes[0], group, slot)
            prob = jnp.sum(hits(routes[0], group) * probs, axis=0, keepdims=True)
            scales.append(jnp.sum(pick * prob, axis=1, keepdims=True))
            picks.append(pick)
        return picks, scales

    picks_a, scales_a = micro(routes_a, logits_a, 0)
    picks_b, scales_b = micro(routes_b, logits_b, CAP)
    place_x[...] = jnp.concatenate(picks_a * 3, axis=0).T.astype(jnp.bfloat16)
    place_u[...] = jnp.concatenate(picks_b * 3, axis=0).T.astype(jnp.bfloat16)
    first = [pick[:LINES] for pick in picks_a]
    pick_x[...] = (first[0] if groups == 1 else jnp.concatenate(first, axis=0)).astype(jnp.bfloat16)
    for group in range(groups):
        scale = scales_a[group] + scales_b[group]
        sum_scale[pl.ds(group * ROWS, ROWS), :] = jnp.broadcast_to(scale, (ROWS, 128))
    stage.wait()


def lines_of(shape, chips):
    line = lax.broadcasted_iota(jnp.int32, shape, 0)
    early = line < chips * LINES
    late = line - chips * LINES
    origin = jnp.where(early, line // LINES, late // FEW)
    slot = jnp.where(early, line % LINES - CAP, CAP - FEW + late % FEW)
    return origin, slot


def pack_half(index, chips, mixed, entry, down, saved, lower, second, factors):
    half = down.shape[2]
    gate = slice(index * half, (index + 1) * half)
    upper = slice((2 + index) * half, (3 + index) * half)
    lower[:, gate] = down[0, 0].T
    turned = entry[0, 0].T
    second[gate, :] = turned[:half]
    second[upper, :] = turned[half:]

    me = lax.axis_index("expert")
    held = saved.shape[2]
    shape = (factors.shape[0], held)
    origin, slot = lines_of(shape, chips)
    if mixed:
        origin = origin ^ (me // CORES)
    wanted = (CORES * origin + me % CORES) * CAP + slot
    wanted = jnp.where(slot >= 0, wanted, -1)
    chosen = jnp.where(wanted == lax.broadcasted_iota(jnp.int32, shape, 1), 1.0, 0.0)
    stored = dot(chosen.astype(jnp.bfloat16), saved[0, 0])
    gates = stored[:, :half]
    uppers = stored[:, half:]
    logistic = jax.nn.sigmoid(gates)
    factors[:, gate] = uppers * logistic * (1.0 + gates * (1.0 - logistic))
    factors[:, upper] = gates * logistic


def pack_own_kernel(chips, mixed, *refs):
    entry_far, down_far, saved_far, entry, down, lower, second, factors, saved, semaphores = refs
    half = down.shape[2]
    rows = second.at[pl.ds(4 * half, half)]
    fetch(
        (entry_far, down_far, saved_far, down_far.at[0, 0]),
        (entry, down, saved, rows),
        semaphores,
    )
    pack_half(0, chips, mixed, entry, down, saved, lower, second, factors)


def pack_pair_kernel(chips, mixed, entry, down, saved, *refs):
    lower, second, factors = refs[3:]
    half = down.shape[2]
    second[5 * half :, :] = down[0, 0]
    pack_half(1, chips, mixed, entry, down, saved, lower, second, factors)


def expert_kernel(chips, *refs):
    arrived = refs[:chips]
    entries = refs[chips : chips + 2]
    lower, second, factors = refs[chips + 2 : chips + 5]
    results = refs[chips + 5 :]
    firsts, fews = zip(*[unfold(ref[...].astype(jnp.float32)) for ref in arrived])
    rows = jnp.concatenate([*firsts, *fews], axis=0).astype(jnp.bfloat16)
    back = dot_by_columns(rows, lower)
    half = back.shape[1] // 2
    grads = jnp.concatenate([back, back], axis=1) * factors[...]
    hidden = []
    for entry in entries:
        made = dot_by_columns(rows, entry.at[0, 0])
        gate = made[:, :half]
        hidden.append(gate * jax.nn.sigmoid(gate) * made[:, half:])
    hidden = jnp.concatenate(hidden, axis=1)
    _, slot = lines_of(hidden.shape, chips)
    hidden = jnp.where(slot < 0, hidden, 0.0)
    inner = jnp.concatenate([grads.astype(jnp.bfloat16), hidden.astype(jnp.bfloat16)], axis=1)
    total = dot(inner, second[...])
    for index, ref in enumerate(results):
        late = chips * LINES + index * FEW
        first = total[index * LINES : (index + 1) * LINES]
        ref[...] = fold(first, total[late : late + FEW]).astype(jnp.bfloat16)


def finish_kernel(groups, chips, *refs):
    x, u, place_x, place_u, sum_scale = refs[:5]
    returned = refs[5 : 5 + chips][::-1]
    out_x, out_u = refs[5 + chips :]
    share = chips // groups
    sums = []
    for group in range(groups):
        total = returned[group * share][...].astype(jnp.float32)
        for ref in returned[group * share + 1 : (group + 1) * share]:
            total = total + ref[...].astype(jnp.float32)
        first, few = unfold(total)
        empty = jnp.zeros((ROWS - 2 * CAP, first.shape[1]), jnp.float32)
        total = jnp.concatenate([first, few, empty], axis=0)
        sums.append(total * sum_scale[pl.ds(group * ROWS, ROWS), :1])
    rest = sums[0] if groups == 1 else jnp.concatenate(sums, axis=0)
    pieces = []
    for _ in range(3):
        piece = rest.astype(jnp.bfloat16)
        pieces.append(piece)
        rest = rest - piece.astype(jnp.float32)
    pieces = jnp.concatenate(pieces, axis=0)
    out_x[0] = (x[0].astype(jnp.float32) + dot(place_x[...], pieces)).astype(jnp.bfloat16)
    out_u[0] = (u[0].astype(jnp.float32) + dot(place_u[...], pieces)).astype(jnp.bfloat16)


def shards(
    section_output,
    section_gradient,
    forward_routes,
    forward_logits,
    backward_routes,
    backward_logits,
    entry_weights,
    down_weights,
    saved_projections,
):
    owners = lax.axis_size("expert")
    groups = owners // FSPLIT
    chips = owners // CORES
    direct = chips == 4
    toks, width = section_output.shape[1:]
    half = down_weights.shape[2]
    shape = jax.ShapeDtypeStruct
    bf16, f32 = jnp.bfloat16, jnp.float32
    routes_a, logits_a, routes_b, logits_b = [
        jnp.swapaxes(value, 1, 2)
        for value in (forward_routes, forward_logits, backward_routes, backward_logits)
    ]

    block = shape((1, toks, width), bf16)
    folded = (LINES, width + width // PARTS)
    asked = along_sections(routes_b, 1)
    layer_input = along_sections(section_output, 1)
    own_values = (routes_a, logits_a, routes_b, logits_b)
    staged, pick_x, place_x, place_u, sum_scale = call(
        functools.partial(prepare_kernel, groups),
        (
            block,
            shape((groups * LINES, toks), bf16),
            shape((toks, 3 * groups * ROWS), bf16),
            shape((toks, 3 * groups * ROWS), bf16),
            shape((groups * ROWS, 128), f32),
        ),
        (),
        8 * MIB,
        10_000_000,
        1_000_000,
        far=(*own_values, section_gradient),
        scratch=[
            *[pltpu.VMEM(value.shape, value.dtype) for value in own_values],
            pltpu.SemaphoreType.DMA((len(own_values),)),
            pltpu.SemaphoreType.DMA((1,)),
        ],
    )
    rows_b = call(
        functools.partial(pick_kernel, groups),
        shape((groups, LINES, width * CAP // LINES), bf16),
        (asked, staged),
        8 * MIB,
        10_000_000_000,
        1_000_000_000,
    )
    weights = (entry_weights, down_weights, saved_projections)
    packs = (
        shape((width, 2 * half), bf16),
        shape((6 * half, width), bf16),
        shape((2 * CAP * chips, 4 * half), f32),
    )
    entry_own, down_own, *packed = call(
        functools.partial(pack_own_kernel, chips, direct),
        (shape(entry_weights.shape, bf16), shape(down_weights.shape, bf16), *packs),
        (),
        8 * MIB,
        10_000_000,
        5_000_000,
        after=(rows_b,),
        far=weights,
        scratch=[
            pltpu.VMEM(saved_projections.shape, bf16),
            pltpu.SemaphoreType.DMA((len(weights) + 1,)),
        ],
    )
    rows_b = along_sections(rows_b, -1)
    weights = [across_owners(value, 1) for value in (entry_own, down_own, saved_projections)]
    message = call(
        functools.partial(merge_kernel, groups),
        shape((groups, *folded), bf16),
        (layer_input, pick_x, rows_b),
        8 * MIB,
        50_000_000_000,
        100_000,
        after=(*packed, weights[2]),
    )
    whole = call(
        release_kernel,
        block,
        (staged,),
        8 * MIB,
        1,
        1,
        after=(message, *weights[:2]),
    )
    upstream = along_sections(whole, -1)
    if direct:
        arrived = [message[0]] + [across_owners(message[0], CORES * flip) for flip in range(1, chips)]
    else:
        same_core = [list(range(core, owners, CORES)) for core in range(CORES)]
        spread = jnp.repeat(message, chips // groups, axis=0)
        gathered = lax.all_to_all(
            spread, "expert", 0, 0, axis_index_groups=same_core, tiled=True
        )
        arrived = [gathered[index] for index in range(chips)]
    packed = call(
        functools.partial(pack_pair_kernel, chips, direct),
        packs,
        (*weights, *packed),
        8 * MIB,
        10_000_000_000,
        5_000_000,
        after=(arrived[-1],),
        aliases={3: 0, 4: 1, 5: 2},
    )
    results = call(
        functools.partial(expert_kernel, chips),
        (shape(folded, bf16),) * chips,
        (*arrived, entry_own, weights[0], *packed),
        16 * MIB,
        800_000_000,
        5_000_000,
    )
    if direct:
        returned = [results[0]] + [
            across_owners(results[flip], CORES * flip) for flip in range(1, chips)
        ]
    else:
        gathered = lax.all_to_all(
            jnp.stack(results), "expert", 0, 0, axis_index_groups=same_core, tiled=True
        )
        returned = [gathered[index] for index in range(chips)]
    return call(
        functools.partial(finish_kernel, groups, chips),
        (block, block),
        (layer_input, upstream, place_x, place_u, sum_scale, *returned[::-1]),
        16 * MIB,
        10_000_000,
        1_000_000,
    )


def solution(mesh):
    rows = P("segment", "expert", None)
    blocks = P("segment", "expert", None, None)
    return jax.shard_map(
        shards,
        mesh=mesh,
        in_specs=(rows,) * 6 + (blocks,) * 3,
        out_specs=(rows, rows),
        check_vma=False,
    )
```

```python
import functools

import jax
import jax.numpy as jnp
from jax import lax
from jax.experimental import pallas as pl
from jax.experimental.pallas import tpu as pltpu
from jax.sharding import PartitionSpec as P

FSPLIT = 8
CAP = 5
CORES = 2
ROWS = 16
LINES = 8
FEW = 2 * CAP - LINES
PARTS = LINES // FEW
MIB = 1 << 20


def along_sections(value, steps):
    count = lax.axis_size("segment")
    pairs = [(source, (source + steps) % count) for source in range(count)]
    return lax.ppermute(value, "segment", pairs)


def across_owners(value, flip):
    count = lax.axis_size("expert")
    return lax.ppermute(value, "expert", [(source, source ^ flip) for source in range(count)])


def call(kernel, outs, args, limit, flops, moved, after=(), aliases=None, far=(), scratch=()):
    whole = pl.BlockSpec(memory_space=pltpu.VMEM)
    anywhere = pl.BlockSpec(memory_space=pl.ANY)
    distant = pl.BlockSpec(memory_space=pltpu.HBM)
    waits = len(after)
    aliases = aliases or {}
    args = [
        pltpu.with_memory_space_constraint(value, pltpu.VMEM) if index in aliases else value
        for index, value in enumerate(args)
    ]

    def body(*refs):
        kernel(*refs[waits:])

    return pl.pallas_call(
        body,
        out_shape=outs,
        in_specs=[anywhere] * waits + [distant] * len(far) + [whole] * len(args),
        out_specs=jax.tree.map(lambda _: whole, outs),
        scratch_shapes=scratch,
        input_output_aliases={
            waits + len(far) + key: value for key, value in aliases.items()
        },
        compiler_params=pltpu.CompilerParams(vmem_limit_bytes=limit),
        cost_estimate=pl.CostEstimate(flops=flops, bytes_accessed=moved, transcendentals=0),
    )(*after, *[pltpu.with_memory_space_constraint(value, pltpu.HBM) for value in far], *args)


def dot(left, right):
    return jnp.dot(left, right, preferred_element_type=jnp.float32)


def dot_by_columns(left, right):
    spans = range(0, right.shape[1], 128)
    return jnp.concatenate([dot(left, right[:, start : start + 128]) for start in spans], axis=1)


def hits(routes, group):
    return jnp.where(routes == group, 1.0, 0.0)


def slot_picks(routes, group, slot):
    rows, toks = slot.shape
    shape = (toks, toks)
    before = lax.broadcasted_iota(jnp.int32, shape, 0) < lax.broadcasted_iota(jnp.int32, shape, 1)
    before = jnp.where(before, 1.0, 0.0).astype(jnp.bfloat16)
    along = jnp.sum(hits(routes, group), axis=0, keepdims=True)
    along = jnp.broadcast_to(along, (rows, toks))
    rank = dot(along.astype(jnp.bfloat16), before)
    return jnp.where(rank == slot.astype(jnp.float32), along, 0.0)


def fold(first, few):
    part = few.shape[1] // PARTS
    few = [few[:, index * part : (index + 1) * part] for index in range(PARTS)]
    return jnp.concatenate([first, jnp.concatenate(few, axis=0)], axis=1)


def runs(width):
    line_width = width * CAP // LINES
    rest = width - line_width
    place, found = 0, []
    while place < CAP * rest:
        row, column = divmod(place, rest)
        line, start = divmod(place, line_width)
        length = min(rest - column, line_width - start)
        found.append((row, line_width + column, CAP + line, start, length))
        place += length
    return line_width, found


def fold_rows(rows):
    line_width, found = runs(rows.shape[1])
    lines = [[] for _ in range(LINES - CAP)]
    for row, column, line, _, length in found:
        lines[line - CAP].append(rows[row : row + 1, column : column + length])
    lines = [jnp.concatenate(parts, axis=1) for parts in lines]
    return jnp.concatenate([rows[:CAP, :line_width], *lines], axis=0)


def unfold_rows(lines, width):
    line_width, found = runs(width)
    rows = [[lines[row : row + 1]] for row in range(CAP)]
    for row, _, line, start, length in found:
        rows[row].append(lines[line : line + 1, start : start + length])
    return jnp.concatenate([jnp.concatenate(parts, axis=1) for parts in rows], axis=0)


def unfold(message):
    width = message.shape[1] * PARTS // (PARTS + 1)
    few = [message[index * FEW : (index + 1) * FEW, width:] for index in range(PARTS)]
    return message[:, :width], jnp.concatenate(few, axis=1)


def fetch(sources, targets, semaphores):
    copies = [
        pltpu.make_async_copy(source, target, semaphores.at[index])
        for index, (source, target) in enumerate(zip(sources, targets))
    ]
    for copy in copies:
        copy.start()
    for copy in copies:
        copy.wait()


def pick_kernel(groups, routes, staged, rows):
    slot = lax.broadcasted_iota(jnp.int32, (LINES, staged.shape[1]), 0)
    for group in range(groups):
        pick = slot_picks(routes[0], group, slot).astype(jnp.bfloat16)
        rows[group] = fold_rows(dot(pick, staged[0])).astype(jnp.bfloat16)


def release_kernel(staged, whole):
    whole[...] = staged[...]


def merge_kernel(groups, x, pick_x, rows_b, message):
    all_a = dot(pick_x[...], x[0])
    for group in range(groups):
        a = all_a[group * LINES : group * LINES + CAP]
        b = unfold_rows(rows_b[group].astype(jnp.float32), x.shape[2])
        first = jnp.concatenate([a, b[: CAP - FEW]], axis=0)
        message[group] = fold(first, b[CAP - FEW :]).astype(jnp.bfloat16)


def prepare_kernel(groups, *refs):
    far, refs = refs[:5], refs[5:]
    staged, pick_x, place_x, place_u, sum_scale = refs[:5]
    near, semaphores, stage_semaphore = refs[5:9], refs[9], refs[10]
    stage = pltpu.make_async_copy(far[4], staged, stage_semaphore.at[0])
    stage.start()
    fetch(far[:4], near, semaphores)
    routes_a, logits_a, routes_b, logits_b = near

    def micro(routes, logits, offset):
        scores = jnp.exp(logits[0])
        probs = scores / jnp.sum(scores, axis=0, keepdims=True)
        slot = lax.broadcasted_iota(jnp.int32, (ROWS, routes.shape[2]), 0) - offset
        picks, scales = [], []
        for group in range(groups):
            pick = slot_picks(routes[0], group, slot)
            prob = jnp.sum(hits(routes[0], group) * probs, axis=0, keepdims=True)
            scales.append(jnp.sum(pick * prob, axis=1, keepdims=True))
            picks.append(pick)
        return picks, scales

    picks_a, scales_a = micro(routes_a, logits_a, 0)
    picks_b, scales_b = micro(routes_b, logits_b, CAP)
    place_x[...] = jnp.concatenate(picks_a * 3, axis=0).T.astype(jnp.bfloat16)
    place_u[...] = jnp.concatenate(picks_b * 3, axis=0).T.astype(jnp.bfloat16)
    first = [pick[:LINES] for pick in picks_a]
    pick_x[...] = (first[0] if groups == 1 else jnp.concatenate(first, axis=0)).astype(jnp.bfloat16)
    for group in range(groups):
        scale = scales_a[group] + scales_b[group]
        sum_scale[pl.ds(group * ROWS, ROWS), :] = jnp.broadcast_to(scale, (ROWS, 128))
    stage.wait()


def lines_of(shape, chips):
    line = lax.broadcasted_iota(jnp.int32, shape, 0)
    early = line < chips * LINES
    late = line - chips * LINES
    origin = jnp.where(early, line // LINES, late // FEW)
    slot = jnp.where(early, line % LINES - CAP, CAP - FEW + late % FEW)
    return origin, slot


def pack_half(index, chips, mixed, entry, down, saved, lower, second, factors):
    half = down.shape[2]
    gate = slice(index * half, (index + 1) * half)
    upper = slice((2 + index) * half, (3 + index) * half)
    lower[:, gate] = down[0, 0].T
    turned = entry[0, 0].T
    second[gate, :] = turned[:half]
    second[upper, :] = turned[half:]

    me = lax.axis_index("expert")
    held = saved.shape[2]
    shape = (factors.shape[0], held)
    origin, slot = lines_of(shape, chips)
    if mixed:
        origin = origin ^ (me // CORES)
    wanted = (CORES * origin + me % CORES) * CAP + slot
    wanted = jnp.where(slot >= 0, wanted, -1)
    chosen = jnp.where(wanted == lax.broadcasted_iota(jnp.int32, shape, 1), 1.0, 0.0)
    stored = dot(chosen.astype(jnp.bfloat16), saved[0, 0])
    gates = stored[:, :half]
    uppers = stored[:, half:]
    logistic = jax.nn.sigmoid(gates)
    factors[:, gate] = uppers * logistic * (1.0 + gates * (1.0 - logistic))
    factors[:, upper] = gates * logistic


def pack_own_kernel(chips, mixed, *refs):
    entry_far, down_far, saved_far, entry, down, lower, second, factors, saved, semaphores = refs
    half = down.shape[2]
    rows = second.at[pl.ds(4 * half, half)]
    fetch(
        (entry_far, down_far, saved_far, down_far.at[0, 0]),
        (entry, down, saved, rows),
        semaphores,
    )
    pack_half(0, chips, mixed, entry, down, saved, lower, second, factors)


def pack_pair_kernel(chips, mixed, entry, down, saved, *refs):
    lower, second, factors = refs[3:]
    half = down.shape[2]
    second[5 * half :, :] = down[0, 0]
    pack_half(1, chips, mixed, entry, down, saved, lower, second, factors)


def expert_kernel(chips, *refs):
    arrived = [refs[0], *refs[chips - 1 : 0 : -1]]
    entries = refs[chips : chips + 2]
    lower, second, factors = refs[chips + 2 : chips + 5]
    results = refs[chips + 5 :]
    firsts, fews = zip(*[unfold(ref[...].astype(jnp.float32)) for ref in arrived])
    rows = jnp.concatenate([*firsts, *fews], axis=0).astype(jnp.bfloat16)
    back = dot_by_columns(rows, lower)
    half = back.shape[1] // 2
    grads = jnp.concatenate([back, back], axis=1) * factors[...]
    hidden = []
    for entry in entries:
        made = dot_by_columns(rows, entry.at[0, 0])
        gate = made[:, :half]
        hidden.append(gate * jax.nn.sigmoid(gate) * made[:, half:])
    hidden = jnp.concatenate(hidden, axis=1)
    _, slot = lines_of(hidden.shape, chips)
    hidden = jnp.where(slot < 0, hidden, 0.0)
    inner = jnp.concatenate([grads.astype(jnp.bfloat16), hidden.astype(jnp.bfloat16)], axis=1)
    total = dot(inner, second[...])
    for index, ref in enumerate(results):
        late = chips * LINES + index * FEW
        first = total[index * LINES : (index + 1) * LINES]
        ref[...] = fold(first, total[late : late + FEW]).astype(jnp.bfloat16)


def finish_kernel(groups, chips, *refs):
    x, u, place_x, place_u, sum_scale = refs[:5]
    returned = refs[5 : 5 + chips][::-1]
    out_x, out_u = refs[5 + chips :]
    share = chips // groups
    sums = []
    for group in range(groups):
        total = returned[group * share][...].astype(jnp.float32)
        for ref in returned[group * share + 1 : (group + 1) * share]:
            total = total + ref[...].astype(jnp.float32)
        first, few = unfold(total)
        empty = jnp.zeros((ROWS - 2 * CAP, first.shape[1]), jnp.float32)
        total = jnp.concatenate([first, few, empty], axis=0)
        sums.append(total * sum_scale[pl.ds(group * ROWS, ROWS), :1])
    rest = sums[0] if groups == 1 else jnp.concatenate(sums, axis=0)
    pieces = []
    for _ in range(3):
        piece = rest.astype(jnp.bfloat16)
        pieces.append(piece)
        rest = rest - piece.astype(jnp.float32)
    pieces = jnp.concatenate(pieces, axis=0)
    out_x[0] = (x[0].astype(jnp.float32) + dot(place_x[...], pieces)).astype(jnp.bfloat16)
    out_u[0] = (u[0].astype(jnp.float32) + dot(place_u[...], pieces)).astype(jnp.bfloat16)


def shards(
    section_output,
    section_gradient,
    forward_routes,
    forward_logits,
    backward_routes,
    backward_logits,
    entry_weights,
    down_weights,
    saved_projections,
):
    owners = lax.axis_size("expert")
    groups = owners // FSPLIT
    chips = owners // CORES
    direct = chips == 4
    toks, width = section_output.shape[1:]
    half = down_weights.shape[2]
    shape = jax.ShapeDtypeStruct
    bf16, f32 = jnp.bfloat16, jnp.float32
    routes_a, logits_a, routes_b, logits_b = [
        jnp.swapaxes(value, 1, 2)
        for value in (forward_routes, forward_logits, backward_routes, backward_logits)
    ]

    block = shape((1, toks, width), bf16)
    folded = (LINES, width + width // PARTS)
    asked = along_sections(routes_b, 1)
    layer_input = along_sections(section_output, 1)
    own_values = (routes_a, logits_a, routes_b, logits_b)
    staged, pick_x, place_x, place_u, sum_scale = call(
        functools.partial(prepare_kernel, groups),
        (
            block,
            shape((groups * LINES, toks), bf16),
            shape((toks, 3 * groups * ROWS), bf16),
            shape((toks, 3 * groups * ROWS), bf16),
            shape((groups * ROWS, 128), f32),
        ),
        (),
        8 * MIB,
        10_000_000,
        1_000_000,
        far=(*own_values, section_gradient),
        scratch=[
            *[pltpu.VMEM(value.shape, value.dtype) for value in own_values],
            pltpu.SemaphoreType.DMA((len(own_values),)),
            pltpu.SemaphoreType.DMA((1,)),
        ],
    )
    rows_b = call(
        functools.partial(pick_kernel, groups),
        shape((groups, LINES, width * CAP // LINES), bf16),
        (asked, staged),
        8 * MIB,
        10_000_000_000,
        1_000_000_000,
    )
    weights = (entry_weights, down_weights, saved_projections)
    packs = (
        shape((width, 2 * half), bf16),
        shape((6 * half, width), bf16),
        shape((2 * CAP * chips, 4 * half), f32),
    )
    entry_own, down_own, *packed = call(
        functools.partial(pack_own_kernel, chips, direct),
        (shape(entry_weights.shape, bf16), shape(down_weights.shape, bf16), *packs),
        (),
        8 * MIB,
        10_000_000,
        5_000_000,
        after=(rows_b,),
        far=weights,
        scratch=[
            pltpu.VMEM(saved_projections.shape, bf16),
            pltpu.SemaphoreType.DMA((len(weights) + 1,)),
        ],
    )
    rows_b = along_sections(rows_b, -1)
    weights = [across_owners(value, 1) for value in (entry_own, down_own, saved_projections)]
    message = call(
        functools.partial(merge_kernel, groups),
        shape((groups, *folded), bf16),
        (layer_input, pick_x, rows_b),
        8 * MIB,
        50_000_000_000,
        100_000,
        after=(*packed, weights[2]),
    )
    whole = call(
        release_kernel,
        block,
        (staged,),
        8 * MIB,
        1,
        1,
        after=(message, *weights[:2]),
    )
    upstream = along_sections(whole, -1)
    if direct:
        arrived = [message[0]] + [across_owners(message[0], CORES * flip) for flip in range(1, chips)]
    else:
        same_core = [list(range(core, owners, CORES)) for core in range(CORES)]
        spread = jnp.repeat(message, chips // groups, axis=0)
        gathered = lax.all_to_all(
            spread, "expert", 0, 0, axis_index_groups=same_core, tiled=True
        )
        arrived = [gathered[index] for index in range(chips)]
    packed = call(
        functools.partial(pack_pair_kernel, chips, direct),
        packs,
        (*weights, *packed),
        8 * MIB,
        10_000_000_000,
        5_000_000,
        after=(arrived[2],),
        aliases={3: 0, 4: 1, 5: 2},
    )
    results = call(
        functools.partial(expert_kernel, chips),
        (shape(folded, bf16),) * chips,
        (arrived[0], *arrived[:0:-1], entry_own, weights[0], *packed),
        16 * MIB,
        800_000_000,
        5_000_000,
    )
    if direct:
        returned = [results[0]] + [
            across_owners(results[flip], CORES * flip) for flip in range(1, chips)
        ]
    else:
        gathered = lax.all_to_all(
            jnp.stack(results), "expert", 0, 0, axis_index_groups=same_core, tiled=True
        )
        returned = [gathered[index] for index in range(chips)]
    return call(
        functools.partial(finish_kernel, groups, chips),
        (block, block),
        (layer_input, upstream, place_x, place_u, sum_scale, *returned[::-1]),
        16 * MIB,
        10_000_000,
        1_000_000,
    )


def solution(mesh):
    rows = P("segment", "expert", None)
    blocks = P("segment", "expert", None, None)
    return jax.shard_map(
        shards,
        mesh=mesh,
        in_specs=(rows,) * 6 + (blocks,) * 3,
        out_specs=(rows, rows),
        check_vma=False,
    )
```

```python
import functools

import jax
import jax.numpy as jnp
from jax import lax
from jax.experimental import pallas as pl
from jax.experimental.pallas import tpu as pltpu
from jax.sharding import PartitionSpec as P

FSPLIT = 8
CAP = 5
CORES = 2
ROWS = 16
LINES = 8
FEW = 2 * CAP - LINES
PARTS = LINES // FEW
MIB = 1 << 20


def along_sections(value, steps):
    count = lax.axis_size("segment")
    pairs = [(source, (source + steps) % count) for source in range(count)]
    return lax.ppermute(value, "segment", pairs)


def across_owners(value, flip):
    count = lax.axis_size("expert")
    return lax.ppermute(value, "expert", [(source, source ^ flip) for source in range(count)])


def call(kernel, outs, args, limit, flops, moved, after=(), aliases=None, far=(), scratch=()):
    whole = pl.BlockSpec(memory_space=pltpu.VMEM)
    anywhere = pl.BlockSpec(memory_space=pl.ANY)
    distant = pl.BlockSpec(memory_space=pltpu.HBM)
    waits = len(after)
    aliases = aliases or {}
    args = [
        pltpu.with_memory_space_constraint(value, pltpu.VMEM) if index in aliases else value
        for index, value in enumerate(args)
    ]

    def body(*refs):
        kernel(*refs[waits:])

    return pl.pallas_call(
        body,
        out_shape=outs,
        in_specs=[anywhere] * waits + [distant] * len(far) + [whole] * len(args),
        out_specs=jax.tree.map(lambda _: whole, outs),
        scratch_shapes=scratch,
        input_output_aliases={
            waits + len(far) + key: value for key, value in aliases.items()
        },
        compiler_params=pltpu.CompilerParams(vmem_limit_bytes=limit),
        cost_estimate=pl.CostEstimate(flops=flops, bytes_accessed=moved, transcendentals=0),
    )(*after, *[pltpu.with_memory_space_constraint(value, pltpu.HBM) for value in far], *args)


def dot(left, right):
    return jnp.dot(left, right, preferred_element_type=jnp.float32)


def dot_by_columns(left, right, step):
    spans = range(0, right.shape[1], step)
    return jnp.concatenate([dot(left, right[:, start : start + step]) for start in spans], axis=1)


def hits(routes, group):
    return jnp.where(routes == group, 1.0, 0.0)


def slot_picks(routes, group, slot):
    rows, toks = slot.shape
    shape = (toks, toks)
    before = lax.broadcasted_iota(jnp.int32, shape, 0) < lax.broadcasted_iota(jnp.int32, shape, 1)
    before = jnp.where(before, 1.0, 0.0).astype(jnp.bfloat16)
    along = jnp.sum(hits(routes, group), axis=0, keepdims=True)
    along = jnp.broadcast_to(along, (rows, toks))
    rank = dot(along.astype(jnp.bfloat16), before)
    return jnp.where(rank == slot.astype(jnp.float32), along, 0.0)


def fold(first, few):
    part = few.shape[1] // PARTS
    few = [few[:, index * part : (index + 1) * part] for index in range(PARTS)]
    return jnp.concatenate([first, jnp.concatenate(few, axis=0)], axis=1)


def runs(width):
    line_width = width * CAP // LINES
    rest = width - line_width
    place, found = 0, []
    while place < CAP * rest:
        row, column = divmod(place, rest)
        line, start = divmod(place, line_width)
        length = min(rest - column, line_width - start)
        found.append((row, line_width + column, CAP + line, start, length))
        place += length
    return line_width, found


def fold_rows(rows):
    line_width, found = runs(rows.shape[1])
    lines = [[] for _ in range(LINES - CAP)]
    for row, column, line, _, length in found:
        lines[line - CAP].append(rows[row : row + 1, column : column + length])
    lines = [jnp.concatenate(parts, axis=1) for parts in lines]
    return jnp.concatenate([rows[:CAP, :line_width], *lines], axis=0)


def unfold_rows(lines, width):
    line_width, found = runs(width)
    rows = [[lines[row : row + 1]] for row in range(CAP)]
    for row, _, line, start, length in found:
        rows[row].append(lines[line : line + 1, start : start + length])
    return jnp.concatenate([jnp.concatenate(parts, axis=1) for parts in rows], axis=0)


def unfold(message):
    width = message.shape[1] * PARTS // (PARTS + 1)
    few = [message[index * FEW : (index + 1) * FEW, width:] for index in range(PARTS)]
    return message[:, :width], jnp.concatenate(few, axis=1)


def fetch(sources, targets, semaphores):
    copies = [
        pltpu.make_async_copy(source, target, semaphores.at[index])
        for index, (source, target) in enumerate(zip(sources, targets))
    ]
    for copy in copies:
        copy.start()
    for copy in copies:
        copy.wait()


def pick_kernel(groups, routes, staged, rows):
    slot = lax.broadcasted_iota(jnp.int32, (LINES, staged.shape[1]), 0)
    for group in range(groups):
        pick = slot_picks(routes[0], group, slot).astype(jnp.bfloat16)
        rows[group] = fold_rows(dot(pick, staged[0])).astype(jnp.bfloat16)


def release_kernel(staged, whole):
    whole[...] = staged[...]


def merge_kernel(groups, x, pick_x, rows_b, message):
    all_a = dot(pick_x[...], x[0])
    for group in range(groups):
        a = all_a[group * LINES : group * LINES + CAP]
        b = unfold_rows(rows_b[group].astype(jnp.float32), x.shape[2])
        first = jnp.concatenate([a, b[: CAP - FEW]], axis=0)
        message[group] = fold(first, b[CAP - FEW :]).astype(jnp.bfloat16)


def prepare_kernel(groups, *refs):
    far, refs = refs[:5], refs[5:]
    staged, pick_x, place_x, place_u, sum_scale = refs[:5]
    near, semaphores, stage_semaphore = refs[5:9], refs[9], refs[10]
    stage = pltpu.make_async_copy(far[4], staged, stage_semaphore.at[0])
    stage.start()
    fetch(far[:4], near, semaphores)
    routes_a, logits_a, routes_b, logits_b = near

    def micro(routes, logits, offset):
        scores = jnp.exp(logits[0])
        probs = scores / jnp.sum(scores, axis=0, keepdims=True)
        slot = lax.broadcasted_iota(jnp.int32, (ROWS, routes.shape[2]), 0) - offset
        picks, scales = [], []
        for group in range(groups):
            pick = slot_picks(routes[0], group, slot)
            prob = jnp.sum(hits(routes[0], group) * probs, axis=0, keepdims=True)
            scales.append(jnp.sum(pick * prob, axis=1, keepdims=True))
            picks.append(pick)
        return picks, scales

    picks_a, scales_a = micro(routes_a, logits_a, 0)
    picks_b, scales_b = micro(routes_b, logits_b, CAP)
    place_x[...] = jnp.concatenate(picks_a * 3, axis=0).T.astype(jnp.bfloat16)
    place_u[...] = jnp.concatenate(picks_b * 3, axis=0).T.astype(jnp.bfloat16)
    first = [pick[:LINES] for pick in picks_a]
    pick_x[...] = (first[0] if groups == 1 else jnp.concatenate(first, axis=0)).astype(jnp.bfloat16)
    for group in range(groups):
        scale = scales_a[group] + scales_b[group]
        sum_scale[pl.ds(group * ROWS, ROWS), :] = jnp.broadcast_to(scale, (ROWS, 128))
    stage.wait()


def lines_of(shape, chips):
    line = lax.broadcasted_iota(jnp.int32, shape, 0)
    early = line < chips * LINES
    late = line - chips * LINES
    origin = jnp.where(early, line // LINES, late // FEW)
    slot = jnp.where(early, line % LINES - CAP, CAP - FEW + late % FEW)
    return origin, slot


def pack_half(index, chips, mixed, entry, down, saved, lower, second, factors):
    half = down.shape[2]
    gate = slice(index * half, (index + 1) * half)
    upper = slice((2 + index) * half, (3 + index) * half)
    lower[:, gate] = down[0, 0].T
    turned = entry[0, 0].T
    second[gate, :] = turned[:half]
    second[upper, :] = turned[half:]

    me = lax.axis_index("expert")
    held = saved.shape[2]
    shape = (factors.shape[0], held)
    origin, slot = lines_of(shape, chips)
    if mixed:
        origin = origin ^ (me // CORES)
    wanted = (CORES * origin + me % CORES) * CAP + slot
    wanted = jnp.where(slot >= 0, wanted, -1)
    chosen = jnp.where(wanted == lax.broadcasted_iota(jnp.int32, shape, 1), 1.0, 0.0)
    stored = dot(chosen.astype(jnp.bfloat16), saved[0, 0])
    gates = stored[:, :half]
    uppers = stored[:, half:]
    logistic = jax.nn.sigmoid(gates)
    factors[:, gate] = uppers * logistic * (1.0 + gates * (1.0 - logistic))
    factors[:, upper] = gates * logistic


def pack_own_kernel(chips, mixed, *refs):
    entry_far, down_far, saved_far, entry, down, lower, second, factors, saved, semaphores = refs
    half = down.shape[2]
    rows = second.at[pl.ds(4 * half, half)]
    fetch(
        (entry_far, down_far, saved_far, down_far.at[0, 0]),
        (entry, down, saved, rows),
        semaphores,
    )
    pack_half(0, chips, mixed, entry, down, saved, lower, second, factors)


def pack_pair_kernel(chips, mixed, entry, down, saved, *refs):
    lower, second, factors = refs[3:]
    half = down.shape[2]
    second[5 * half :, :] = down[0, 0]
    pack_half(1, chips, mixed, entry, down, saved, lower, second, factors)


def expert_kernel(chips, *refs):
    arrived = [refs[0], *refs[chips - 1 : 0 : -1]]
    entries = refs[chips : chips + 2]
    lower, second, factors = refs[chips + 2 : chips + 5]
    results = refs[chips + 5 :]
    firsts, fews = zip(*[unfold(ref[...].astype(jnp.float32)) for ref in arrived])
    rows = jnp.concatenate([*firsts, *fews], axis=0).astype(jnp.bfloat16)
    back = dot_by_columns(rows, lower, 128)
    half = back.shape[1] // 2
    grads = jnp.concatenate([back, back], axis=1) * factors[...]
    hidden = []
    for entry in entries:
        made = dot_by_columns(rows, entry.at[0, 0], 128)
        gate = made[:, :half]
        hidden.append(gate * jax.nn.sigmoid(gate) * made[:, half:])
    hidden = jnp.concatenate(hidden, axis=1)
    _, slot = lines_of(hidden.shape, chips)
    hidden = jnp.where(slot < 0, hidden, 0.0)
    inner = jnp.concatenate([grads.astype(jnp.bfloat16), hidden.astype(jnp.bfloat16)], axis=1)
    total = dot_by_columns(inner, second, 256)
    for index, ref in enumerate(results):
        late = chips * LINES + index * FEW
        first = total[index * LINES : (index + 1) * LINES]
        ref[...] = fold(first, total[late : late + FEW]).astype(jnp.bfloat16)


def finish_kernel(groups, chips, *refs):
    x, u, place_x, place_u, sum_scale = refs[:5]
    returned = refs[5 : 5 + chips][::-1]
    out_x, out_u = refs[5 + chips :]
    share = chips // groups
    sums = []
    for group in range(groups):
        total = returned[group * share][...].astype(jnp.float32)
        for ref in returned[group * share + 1 : (group + 1) * share]:
            total = total + ref[...].astype(jnp.float32)
        first, few = unfold(total)
        empty = jnp.zeros((ROWS - 2 * CAP, first.shape[1]), jnp.float32)
        total = jnp.concatenate([first, few, empty], axis=0)
        sums.append(total * sum_scale[pl.ds(group * ROWS, ROWS), :1])
    rest = sums[0] if groups == 1 else jnp.concatenate(sums, axis=0)
    pieces = []
    for _ in range(3):
        piece = rest.astype(jnp.bfloat16)
        pieces.append(piece)
        rest = rest - piece.astype(jnp.float32)
    pieces = jnp.concatenate(pieces, axis=0)
    out_x[0] = (x[0].astype(jnp.float32) + dot(place_x[...], pieces)).astype(jnp.bfloat16)
    out_u[0] = (u[0].astype(jnp.float32) + dot(place_u[...], pieces)).astype(jnp.bfloat16)


def shards(
    section_output,
    section_gradient,
    forward_routes,
    forward_logits,
    backward_routes,
    backward_logits,
    entry_weights,
    down_weights,
    saved_projections,
):
    owners = lax.axis_size("expert")
    groups = owners // FSPLIT
    chips = owners // CORES
    direct = chips == 4
    toks, width = section_output.shape[1:]
    half = down_weights.shape[2]
    shape = jax.ShapeDtypeStruct
    bf16, f32 = jnp.bfloat16, jnp.float32
    routes_a, logits_a, routes_b, logits_b = [
        jnp.swapaxes(value, 1, 2)
        for value in (forward_routes, forward_logits, backward_routes, backward_logits)
    ]

    block = shape((1, toks, width), bf16)
    folded = (LINES, width + width // PARTS)
    asked = along_sections(routes_b, 1)
    layer_input = along_sections(section_output, 1)
    own_values = (routes_a, logits_a, routes_b, logits_b)
    staged, pick_x, place_x, place_u, sum_scale = call(
        functools.partial(prepare_kernel, groups),
        (
            block,
            shape((groups * LINES, toks), bf16),
            shape((toks, 3 * groups * ROWS), bf16),
            shape((toks, 3 * groups * ROWS), bf16),
            shape((groups * ROWS, 128), f32),
        ),
        (),
        8 * MIB,
        10_000_000,
        1_000_000,
        far=(*own_values, section_gradient),
        scratch=[
            *[pltpu.VMEM(value.shape, value.dtype) for value in own_values],
            pltpu.SemaphoreType.DMA((len(own_values),)),
            pltpu.SemaphoreType.DMA((1,)),
        ],
    )
    rows_b = call(
        functools.partial(pick_kernel, groups),
        shape((groups, LINES, width * CAP // LINES), bf16),
        (asked, staged),
        8 * MIB,
        10_000_000_000,
        1_000_000_000,
    )
    weights = (entry_weights, down_weights, saved_projections)
    packs = (
        shape((width, 2 * half), bf16),
        shape((6 * half, width), bf16),
        shape((2 * CAP * chips, 4 * half), f32),
    )
    entry_own, down_own, *packed = call(
        functools.partial(pack_own_kernel, chips, direct),
        (shape(entry_weights.shape, bf16), shape(down_weights.shape, bf16), *packs),
        (),
        8 * MIB,
        10_000_000,
        5_000_000,
        after=(rows_b,),
        far=weights,
        scratch=[
            pltpu.VMEM(saved_projections.shape, bf16),
            pltpu.SemaphoreType.DMA((len(weights) + 1,)),
        ],
    )
    rows_b = along_sections(rows_b, -1)
    weights = [across_owners(value, 1) for value in (entry_own, down_own, saved_projections)]
    message = call(
        functools.partial(merge_kernel, groups),
        shape((groups, *folded), bf16),
        (layer_input, pick_x, rows_b),
        8 * MIB,
        50_000_000_000,
        100_000,
        after=(*packed, weights[2]),
    )
    whole = call(
        release_kernel,
        block,
        (staged,),
        8 * MIB,
        1,
        1,
        after=(message, *weights[:2]),
    )
    upstream = along_sections(whole, -1)
    if direct:
        arrived = [message[0]] + [across_owners(message[0], CORES * flip) for flip in range(1, chips)]
    else:
        same_core = [list(range(core, owners, CORES)) for core in range(CORES)]
        spread = jnp.repeat(message, chips // groups, axis=0)
        gathered = lax.all_to_all(
            spread, "expert", 0, 0, axis_index_groups=same_core, tiled=True
        )
        arrived = [gathered[index] for index in range(chips)]
    packed = call(
        functools.partial(pack_pair_kernel, chips, direct),
        packs,
        (*weights, *packed),
        8 * MIB,
        10_000_000_000,
        5_000_000,
        after=(arrived[2],),
        aliases={3: 0, 4: 1, 5: 2},
    )
    results = call(
        functools.partial(expert_kernel, chips),
        (shape(folded, bf16),) * chips,
        (arrived[0], *arrived[:0:-1], entry_own, weights[0], *packed),
        16 * MIB,
        800_000_000,
        5_000_000,
    )
    if direct:
        returned = [results[0]] + [
            across_owners(results[flip], CORES * flip) for flip in range(1, chips)
        ]
    else:
        gathered = lax.all_to_all(
            jnp.stack(results), "expert", 0, 0, axis_index_groups=same_core, tiled=True
        )
        returned = [gathered[index] for index in range(chips)]
    return call(
        functools.partial(finish_kernel, groups, chips),
        (block, block),
        (layer_input, upstream, place_x, place_u, sum_scale, *returned[::-1]),
        16 * MIB,
        10_000_000,
        1_000_000,
    )


def solution(mesh):
    rows = P("segment", "expert", None)
    blocks = P("segment", "expert", None, None)
    return jax.shard_map(
        shards,
        mesh=mesh,
        in_specs=(rows,) * 6 + (blocks,) * 3,
        out_specs=(rows, rows),
        check_vma=False,
    )
```

```python
import functools

import jax
import jax.numpy as jnp
from jax import lax
from jax.experimental import pallas as pl
from jax.experimental.pallas import tpu as pltpu
from jax.sharding import PartitionSpec as P

FSPLIT = 8
CAP = 5
CORES = 2
ROWS = 16
LINES = 8
FEW = 2 * CAP - LINES
PARTS = LINES // FEW
MIB = 1 << 20


def along_sections(value, steps):
    count = lax.axis_size("segment")
    pairs = [(source, (source + steps) % count) for source in range(count)]
    return lax.ppermute(value, "segment", pairs)


def across_owners(value, flip):
    count = lax.axis_size("expert")
    return lax.ppermute(value, "expert", [(source, source ^ flip) for source in range(count)])


def call(kernel, outs, args, limit, flops, moved, after=(), aliases=None, far=(), scratch=()):
    whole = pl.BlockSpec(memory_space=pltpu.VMEM)
    anywhere = pl.BlockSpec(memory_space=pl.ANY)
    distant = pl.BlockSpec(memory_space=pltpu.HBM)
    waits = len(after)
    aliases = aliases or {}
    args = [
        pltpu.with_memory_space_constraint(value, pltpu.VMEM) if index in aliases else value
        for index, value in enumerate(args)
    ]

    def body(*refs):
        kernel(*refs[waits:])

    return pl.pallas_call(
        body,
        out_shape=outs,
        in_specs=[anywhere] * waits + [distant] * len(far) + [whole] * len(args),
        out_specs=jax.tree.map(lambda _: whole, outs),
        scratch_shapes=scratch,
        input_output_aliases={
            waits + len(far) + key: value for key, value in aliases.items()
        },
        compiler_params=pltpu.CompilerParams(vmem_limit_bytes=limit),
        cost_estimate=pl.CostEstimate(flops=flops, bytes_accessed=moved, transcendentals=0),
    )(*after, *[pltpu.with_memory_space_constraint(value, pltpu.HBM) for value in far], *args)


def dot(left, right):
    return jnp.dot(left, right, preferred_element_type=jnp.float32)


def dot_by_columns(left, right):
    spans = range(0, right.shape[1], 128)
    return jnp.concatenate([dot(left, right[:, start : start + 128]) for start in spans], axis=1)


def hits(routes, group):
    return jnp.where(routes == group, 1.0, 0.0)


def slot_picks(routes, group, slot):
    rows, toks = slot.shape
    shape = (toks, toks)
    before = lax.broadcasted_iota(jnp.int32, shape, 0) < lax.broadcasted_iota(jnp.int32, shape, 1)
    before = jnp.where(before, 1.0, 0.0).astype(jnp.bfloat16)
    along = jnp.sum(hits(routes, group), axis=0, keepdims=True)
    along = jnp.broadcast_to(along, (rows, toks))
    rank = dot(along.astype(jnp.bfloat16), before)
    return jnp.where(rank == slot.astype(jnp.float32), along, 0.0)


def fold(first, few):
    part = few.shape[1] // PARTS
    few = [few[:, index * part : (index + 1) * part] for index in range(PARTS)]
    return jnp.concatenate([first, jnp.concatenate(few, axis=0)], axis=1)


def runs(width):
    line_width = width * CAP // LINES
    rest = width - line_width
    place, found = 0, []
    while place < CAP * rest:
        row, column = divmod(place, rest)
        line, start = divmod(place, line_width)
        length = min(rest - column, line_width - start)
        found.append((row, line_width + column, CAP + line, start, length))
        place += length
    return line_width, found


def fold_rows(rows):
    line_width, found = runs(rows.shape[1])
    lines = [[] for _ in range(LINES - CAP)]
    for row, column, line, _, length in found:
        lines[line - CAP].append(rows[row : row + 1, column : column + length])
    lines = [jnp.concatenate(parts, axis=1) for parts in lines]
    return jnp.concatenate([rows[:CAP, :line_width], *lines], axis=0)


def unfold_rows(lines, width):
    line_width, found = runs(width)
    rows = [[lines[row : row + 1]] for row in range(CAP)]
    for row, _, line, start, length in found:
        rows[row].append(lines[line : line + 1, start : start + length])
    return jnp.concatenate([jnp.concatenate(parts, axis=1) for parts in rows], axis=0)


def unfold(message):
    width = message.shape[1] * PARTS // (PARTS + 1)
    few = [message[index * FEW : (index + 1) * FEW, width:] for index in range(PARTS)]
    return message[:, :width], jnp.concatenate(few, axis=1)


def fetch(sources, targets, semaphores):
    copies = [
        pltpu.make_async_copy(source, target, semaphores.at[index])
        for index, (source, target) in enumerate(zip(sources, targets))
    ]
    for copy in copies:
        copy.start()
    for copy in copies:
        copy.wait()


def pick_kernel(groups, routes, staged, rows):
    slot = lax.broadcasted_iota(jnp.int32, (LINES, staged.shape[1]), 0)
    for group in range(groups):
        pick = slot_picks(routes[0], group, slot).astype(jnp.bfloat16)
        rows[group] = fold_rows(dot(pick, staged[0])).astype(jnp.bfloat16)


def release_kernel(staged, whole):
    whole[...] = staged[...]


def merge_kernel(groups, x, pick_x, rows_b, message):
    all_a = dot(pick_x[...], x[0])
    for group in range(groups):
        a = all_a[group * LINES : group * LINES + CAP]
        b = unfold_rows(rows_b[group].astype(jnp.float32), x.shape[2])
        first = jnp.concatenate([a, b[: CAP - FEW]], axis=0)
        message[group] = fold(first, b[CAP - FEW :]).astype(jnp.bfloat16)


def prepare_kernel(groups, *refs):
    far, refs = refs[:5], refs[5:]
    staged, pick_x, place_x, place_u, sum_scale = refs[:5]
    near, semaphores, stage_semaphore = refs[5:9], refs[9], refs[10]
    stage = pltpu.make_async_copy(far[4], staged, stage_semaphore.at[0])
    stage.start()
    fetch(far[:4], near, semaphores)
    routes_a, logits_a, routes_b, logits_b = near

    def micro(routes, logits, offset):
        scores = jnp.exp(logits[0])
        probs = scores / jnp.sum(scores, axis=0, keepdims=True)
        slot = lax.broadcasted_iota(jnp.int32, (ROWS, routes.shape[2]), 0) - offset
        picks, scales = [], []
        for group in range(groups):
            pick = slot_picks(routes[0], group, slot)
            prob = jnp.sum(hits(routes[0], group) * probs, axis=0, keepdims=True)
            scales.append(jnp.sum(pick * prob, axis=1, keepdims=True))
            picks.append(pick)
        return picks, scales

    picks_a, scales_a = micro(routes_a, logits_a, 0)
    picks_b, scales_b = micro(routes_b, logits_b, CAP)
    place_x[...] = jnp.concatenate(picks_a * 3, axis=0).T.astype(jnp.bfloat16)
    place_u[...] = jnp.concatenate(picks_b * 3, axis=0).T.astype(jnp.bfloat16)
    first = [pick[:LINES] for pick in picks_a]
    pick_x[...] = (first[0] if groups == 1 else jnp.concatenate(first, axis=0)).astype(jnp.bfloat16)
    for group in range(groups):
        scale = scales_a[group] + scales_b[group]
        sum_scale[pl.ds(group * ROWS, ROWS), :] = jnp.broadcast_to(scale, (ROWS, 128))
    stage.wait()


def lines_of(shape, chips):
    line = lax.broadcasted_iota(jnp.int32, shape, 0)
    early = line < chips * LINES
    late = line - chips * LINES
    origin = jnp.where(early, line // LINES, late // FEW)
    slot = jnp.where(early, line % LINES - CAP, CAP - FEW + late % FEW)
    return origin, slot


def pack_half(index, chips, mixed, entry, down, saved, lower, second, factors):
    half = down.shape[2]
    gate = slice(index * half, (index + 1) * half)
    upper = slice((2 + index) * half, (3 + index) * half)
    lower[:, gate] = down[0, 0].T
    turned = entry[0, 0].T
    second[gate, :] = turned[:half]
    second[upper, :] = turned[half:]

    me = lax.axis_index("expert")
    held = saved.shape[2]
    shape = (factors.shape[0], held)
    origin, slot = lines_of(shape, chips)
    if mixed:
        origin = origin ^ (me // CORES)
    wanted = (CORES * origin + me % CORES) * CAP + slot
    wanted = jnp.where(slot >= 0, wanted, -1)
    chosen = jnp.where(wanted == lax.broadcasted_iota(jnp.int32, shape, 1), 1.0, 0.0)
    stored = dot(chosen.astype(jnp.bfloat16), saved[0, 0])
    gates = stored[:, :half]
    uppers = stored[:, half:]
    logistic = jax.nn.sigmoid(gates)
    factors[:, gate] = uppers * logistic * (1.0 + gates * (1.0 - logistic))
    factors[:, upper] = gates * logistic


def pack_own_kernel(chips, mixed, *refs):
    entry_far, down_far, saved_far, entry, down, lower, second, factors, saved, semaphores = refs
    half = down.shape[2]
    rows = second.at[pl.ds(4 * half, half)]
    fetch(
        (entry_far, down_far, saved_far, down_far.at[0, 0]),
        (entry, down, saved, rows),
        semaphores,
    )
    pack_half(0, chips, mixed, entry, down, saved, lower, second, factors)


def pack_pair_kernel(chips, mixed, entry, down, saved, *refs):
    lower, second, factors = refs[3:]
    half = down.shape[2]
    second[5 * half :, :] = down[0, 0]
    pack_half(1, chips, mixed, entry, down, saved, lower, second, factors)


def expert_kernel(chips, *refs):
    arrived = [refs[0], *refs[chips - 1 : 0 : -1]]
    entries = refs[chips : chips + 2]
    lower, second, factors = refs[chips + 2 : chips + 5]
    results = refs[chips + 5 :]
    firsts, fews = zip(*[unfold(ref[...].astype(jnp.float32)) for ref in arrived])
    rows = jnp.concatenate([*firsts, *fews], axis=0).astype(jnp.bfloat16)
    back = dot_by_columns(rows, lower)
    half = back.shape[1] // 2
    grads = jnp.concatenate([back, back], axis=1) * factors[...]
    hidden = []
    for entry in entries:
        made = dot_by_columns(rows, entry.at[0, 0])
        gate = made[:, :half]
        hidden.append(gate * jax.nn.sigmoid(gate) * made[:, half:])
    hidden = jnp.concatenate(hidden, axis=1)
    _, slot = lines_of(hidden.shape, chips)
    hidden = jnp.where(slot < 0, hidden, 0.0)
    inner = jnp.concatenate([grads.astype(jnp.bfloat16), hidden.astype(jnp.bfloat16)], axis=1)
    cut = second.shape[1] // 2
    total = jnp.concatenate([dot(inner, second[:, :cut]), dot(inner, second[:, cut:])], axis=1)
    for index, ref in enumerate(results):
        late = chips * LINES + index * FEW
        first = total[index * LINES : (index + 1) * LINES]
        ref[...] = fold(first, total[late : late + FEW]).astype(jnp.bfloat16)


def finish_kernel(groups, chips, *refs):
    x, u, place_x, place_u, sum_scale = refs[:5]
    returned = refs[5 : 5 + chips]
    if chips == 4:
        returned = [returned[k] for k in [3, 2, 0, 1]]
    out_x, out_u = refs[5 + chips :]
    share = chips // groups
    sums = []
    for group in range(groups):
        total = returned[group * share][...].astype(jnp.float32)
        for ref in returned[group * share + 1 : (group + 1) * share]:
            total = total + ref[...].astype(jnp.float32)
        first, few = unfold(total)
        empty = jnp.zeros((ROWS - 2 * CAP, first.shape[1]), jnp.float32)
        total = jnp.concatenate([first, few, empty], axis=0)
        sums.append(total * sum_scale[pl.ds(group * ROWS, ROWS), :1])
    rest = sums[0] if groups == 1 else jnp.concatenate(sums, axis=0)
    pieces = []
    for _ in range(3):
        piece = rest.astype(jnp.bfloat16)
        pieces.append(piece)
        rest = rest - piece.astype(jnp.float32)
    pieces = jnp.concatenate(pieces, axis=0)
    out_x[0] = (x[0].astype(jnp.float32) + dot(place_x[...], pieces)).astype(jnp.bfloat16)
    out_u[0] = (u[0].astype(jnp.float32) + dot(place_u[...], pieces)).astype(jnp.bfloat16)


def shards(
    section_output,
    section_gradient,
    forward_routes,
    forward_logits,
    backward_routes,
    backward_logits,
    entry_weights,
    down_weights,
    saved_projections,
):
    owners = lax.axis_size("expert")
    groups = owners // FSPLIT
    chips = owners // CORES
    direct = chips == 4
    toks, width = section_output.shape[1:]
    half = down_weights.shape[2]
    shape = jax.ShapeDtypeStruct
    bf16, f32 = jnp.bfloat16, jnp.float32
    routes_a, logits_a, routes_b, logits_b = [
        jnp.swapaxes(value, 1, 2)
        for value in (forward_routes, forward_logits, backward_routes, backward_logits)
    ]

    block = shape((1, toks, width), bf16)
    folded = (LINES, width + width // PARTS)
    asked = along_sections(routes_b, 1)
    layer_input = along_sections(section_output, 1)
    own_values = (routes_a, logits_a, routes_b, logits_b)
    staged, pick_x, place_x, place_u, sum_scale = call(
        functools.partial(prepare_kernel, groups),
        (
            block,
            shape((groups * LINES, toks), bf16),
            shape((toks, 3 * groups * ROWS), bf16),
            shape((toks, 3 * groups * ROWS), bf16),
            shape((groups * ROWS, 128), f32),
        ),
        (),
        8 * MIB,
        10_000_000,
        1_000_000,
        far=(*own_values, section_gradient),
        scratch=[
            *[pltpu.VMEM(value.shape, value.dtype) for value in own_values],
            pltpu.SemaphoreType.DMA((len(own_values),)),
            pltpu.SemaphoreType.DMA((1,)),
        ],
    )
    rows_b = call(
        functools.partial(pick_kernel, groups),
        shape((groups, LINES, width * CAP // LINES), bf16),
        (asked, staged),
        8 * MIB,
        10_000_000_000,
        1_000_000_000,
    )
    weights = (entry_weights, down_weights, saved_projections)
    packs = (
        shape((width, 2 * half), bf16),
        shape((6 * half, width), bf16),
        shape((2 * CAP * chips, 4 * half), f32),
    )
    entry_own, down_own, *packed = call(
        functools.partial(pack_own_kernel, chips, direct),
        (shape(entry_weights.shape, bf16), shape(down_weights.shape, bf16), *packs),
        (),
        8 * MIB,
        10_000_000,
        5_000_000,
        after=(rows_b,),
        far=weights,
        scratch=[
            pltpu.VMEM(saved_projections.shape, bf16),
            pltpu.SemaphoreType.DMA((len(weights) + 1,)),
        ],
    )
    rows_b = along_sections(rows_b, -1)
    weights = [across_owners(value, 1) for value in (entry_own, down_own, saved_projections)]
    message = call(
        functools.partial(merge_kernel, groups),
        shape((groups, *folded), bf16),
        (layer_input, pick_x, rows_b),
        8 * MIB,
        50_000_000_000,
        100_000,
        after=(*packed, weights[2]),
    )
    whole = call(
        release_kernel,
        block,
        (staged,),
        8 * MIB,
        1,
        1,
        after=(message, *weights[:2]),
    )
    upstream = along_sections(whole, -1)
    if direct:
        arrived = [message[0]] + [across_owners(message[0], CORES * flip) for flip in range(1, chips)]
    else:
        same_core = [list(range(core, owners, CORES)) for core in range(CORES)]
        spread = jnp.repeat(message, chips // groups, axis=0)
        gathered = lax.all_to_all(
            spread, "expert", 0, 0, axis_index_groups=same_core, tiled=True
        )
        arrived = [gathered[index] for index in range(chips)]
    packed = call(
        functools.partial(pack_pair_kernel, chips, direct),
        packs,
        (*weights, *packed),
        8 * MIB,
        10_000_000_000,
        5_000_000,
        after=(arrived[2],),
        aliases={3: 0, 4: 1, 5: 2},
    )
    results = call(
        functools.partial(expert_kernel, chips),
        (shape(folded, bf16),) * chips,
        (arrived[0], *arrived[:0:-1], entry_own, weights[0], *packed),
        16 * MIB,
        800_000_000,
        5_000_000,
    )
    if direct:
        returned = [results[0]] + [
            across_owners(results[flip], CORES * flip) for flip in range(1, chips)
        ]
    else:
        gathered = lax.all_to_all(
            jnp.stack(results), "expert", 0, 0, axis_index_groups=same_core, tiled=True
        )
        returned = [gathered[index] for index in range(chips)]
    return call(
        functools.partial(finish_kernel, groups, chips),
        (block, block),
        (layer_input, upstream, place_x, place_u, sum_scale, *([returned[k] for k in (2, 3, 1, 0)] if direct else returned)),
        16 * MIB,
        10_000_000,
        1_000_000,
    )


def solution(mesh):
    rows = P("segment", "expert", None)
    blocks = P("segment", "expert", None, None)
    return jax.shard_map(
        shards,
        mesh=mesh,
        in_specs=(rows,) * 6 + (blocks,) * 3,
        out_specs=(rows, rows),
        check_vma=False,
    )
```
